32 devices in a mesh: dp: 4 (over y, x), ctx: 8 (over z, core).
Axes of the slice: x: 2, y: 2, z: 4, core: 2. Of those that a mesh axis runs over, the one named last changes fastest.
Arguments:
- projected: bfloat16 [4, 1024, 12288], P('dp', 'ctx'), may hold values from -6 to 6
- doc_ids: int32 [4, 1024], P('dp'), may hold values from 0 to 15, never falling along the last dimension, each value on 1 to 128 neighbouring positions
- short_filter: float32 [3, 12288], replicated, may hold values from -3.5 to 3.5
- long_filter: bfloat16 [256, 128], replicated, may hold values from -0.5 to 0.5
- cotangent: bfloat16 [4, 1024, 4096], P('dp', 'ctx'), may hold values from -6 to 6
Outputs:
- block_out: bfloat16 [4, 1024, 4096], P('dp', 'ctx')
- grad_projected: bfloat16 [4, 1024, 12288], P('dp', 'ctx')
- grad_short: float32 [3, 12288], P(None, 'ctx')
- grad_long: float32 [256, 128], P('ctx')
The draws below stay inside these ranges and needn't reach their ends.
Inputs may be any that keep to these rules, and one draw needn't show every extreme that they name: `doc_ids`: document numbers never fall along a row, each document spans 1 to 128 positions, and some document spans exactly 128.
All inputs are finite; a program needn't handle non-finite values.
Results may differ from the reference program's by a relative error of at most 0.0076.
Values may be sent and summed in bfloat16 or wider, within the bound.
No kernel may reach another device: no remote copies, remote signals or barrier semaphores. Data moves between devices by JAX's collectives and lax.ppermute only.
A program may use at most 256 MiB of HBM per device.

```python
import math
import jax
import jax.numpy as jnp
import numpy as np
from jax import lax

D = 4096
SHORT_TAPS = 3
MED_TAPS = 128
DOCS = 16
GROUPS = 256
WINDOW = 1024
DOC_MOST = 128
BATCH = 4
N_DP = 4


def levels(stream_key, shape, cuts, smallest, high):
    def one(position, parts):
        steps = jax.random.uniform(jax.random.fold_in(jax.random.fold_in(stream_key, 6), position), (parts,), jnp.float32, smallest / len(cuts), high / len(cuts))
        return jnp.repeat(jnp.exp(steps), shape[position] // parts).reshape((-1,) + (1,) * (len(shape) - position - 1))

    level = one(*cuts[0])
    for cut in cuts[1:]:
        level = level * one(*cut)
    return level


def profile(count, total, limit, skew):
    portions = [(1 << 20) // math.isqrt(standing ** skew) + 1 for standing in range(2, count + 1)]
    surplus, given = total - limit - (count - 1), [1] * (count - 1)
    while surplus > 0:
        free = [i for i in range(count - 1) if given[i] < limit]
        mass, left = sum([portions[i] for i in free]), surplus
        for i in free:
            more = min(limit - given[i], max(1, left * portions[i] // mass), surplus)
            given[i] = given[i] + more
            surplus = surplus - more
    return np.array([limit] + given)


def uneven_parts(own_key, amount, total, reach, lean):
    if amount == 2:
        one = jax.random.randint(own_key, (), max(1, total - reach), min(reach, total - 1) + 1)
        return jnp.stack([one, total - one])
    tallies = jnp.asarray(profile(amount, total, reach, lean), jnp.int32)
    twos = (amount - 1) // 2
    giver, taker = tallies[1:1 + 2 * twos:2], tallies[2:2 + 2 * twos:2]
    margin = jnp.minimum(giver - 1, reach - taker)
    passed = jax.random.randint(jax.random.fold_in(own_key, 1), (twos,), 0, 1 << 20) % (margin + 1)
    tallies = tallies.at[1:1 + 2 * twos:2].set(giver - passed).at[2:2 + 2 * twos:2].set(taker + passed)
    return tallies[jax.random.permutation(jax.random.fold_in(own_key, 2), amount)]


def normal_values(stream_key, shape, deviation, reach, shards=(), kind=jnp.bfloat16):
    drawn = deviation * jax.random.normal(stream_key, shape, jnp.float32)
    if shards:
        drawn = drawn * levels(stream_key, shape, shards, -0.22, 0.18)
    return jnp.clip(drawn, -reach, reach).astype(kind)


def setup_inputs(seed: int = 0) -> dict:
    keys = jax.random.split(jax.random.key(seed), 6)
    projected = normal_values(keys[0], (BATCH, WINDOW, 3 * D), 1.0, 6.0, ((0, 4), (1, 8)))
    doc_ids = jax.vmap(lambda own: jnp.searchsorted(jnp.cumsum(uneven_parts(own, DOCS, WINDOW, DOC_MOST, 2)), jnp.arange(WINDOW), side="right"))(jax.random.split(keys[1], BATCH)).reshape((BATCH, WINDOW)).astype(jnp.int32)
    short_filter = normal_values(keys[2], (SHORT_TAPS, 3 * D), SHORT_TAPS ** -0.5, 3.5, (), jnp.float32)
    long_filter = normal_values(keys[3], (GROUPS, MED_TAPS), MED_TAPS ** -0.5, 0.5)
    cotangent = normal_values(keys[4], (BATCH, WINDOW, D), 1.0, 6.0, ((0, 4), (1, 8)))
    return dict(projected=projected, doc_ids=doc_ids, short_filter=short_filter, long_filter=long_filter, cotangent=cotangent)


def doc_offsets(seg_row):
    length = seg_row.shape[0]
    places = jnp.arange(length, dtype=jnp.int32)
    starts_here = jnp.concatenate([jnp.ones((1,), bool), seg_row[1:] != seg_row[:-1]])
    return (places - lax.cummax(jnp.where(starts_here, places, 0), axis=0)).astype(jnp.int32)

def toeplitz(filters):
    groups, tap_count = filters.shape
    widened = jnp.concatenate([jnp.zeros((groups, tap_count), filters.dtype), filters[:, ::-1], jnp.zeros((groups, tap_count - 1), filters.dtype)], axis=1)
    tiled_rows = jnp.tile(widened, (1, tap_count))
    span_len = 3 * tap_count - 2
    return tiled_rows[:, tap_count - 1:tap_count - 1 + tap_count * span_len].reshape(groups, tap_count, span_len)[:, :, :2 * tap_count]

def short_forward(extended, weights, offsets):
    short_taps = weights.shape[0]
    tok_count = offsets.shape[0]
    running = jnp.zeros((tok_count, extended.shape[1]), jnp.float32)
    for tap_pos in range(short_taps):
        shifted = extended[short_taps - 1 - tap_pos:short_taps - 1 - tap_pos + tok_count].astype(jnp.float32)
        running = running + jnp.where((offsets >= tap_pos)[:, None], weights[tap_pos][None, :] * shifted, 0.0)
    return running

def short_backward(grads_ext, offsets_ext, extended, weights, offsets):
    short_taps = weights.shape[0]
    tok_count = offsets.shape[0]
    running = jnp.zeros((tok_count, extended.shape[1]), jnp.float32)
    pieces = []
    for tap_pos in range(short_taps):
        ahead_part = grads_ext[tap_pos:tap_pos + tok_count].astype(jnp.float32)
        keep_mask = (offsets_ext[tap_pos:tap_pos + tok_count] >= tap_pos)[:, None]
        running = running + jnp.where(keep_mask, weights[tap_pos][None, :] * ahead_part, 0.0)
        shifted = extended[short_taps - 1 - tap_pos:short_taps - 1 - tap_pos + tok_count].astype(jnp.float32)
        local_grad = grads_ext[:tok_count].astype(jnp.float32)
        pieces.append(lax.optimization_barrier(jnp.sum(jnp.where((offsets >= tap_pos)[:, None], local_grad * shifted, 0.0), axis=0)))
    return (running, jnp.stack(pieces, axis=0))

def reference(projected, doc_ids, short_filter, long_filter, cotangent):
    kernel = toeplitz(long_filter).astype(jnp.float32)
    groups, tap_count = long_filter.shape
    model_width = cotangent.shape[2]
    length = projected.shape[1]
    blocks = length // tap_count
    short_taps = short_filter.shape[0]
    row_ids = jnp.arange(tap_count, dtype=jnp.int32)[:, None]
    col_ids = jnp.arange(2 * tap_count, dtype=jnp.int32)[None, :]

    def one_window(window_items):
        inputs_row, seg_row, grad_row = window_items
        offsets = doc_offsets(seg_row)
        extended = jnp.concatenate([jnp.zeros((short_taps - 1, inputs_row.shape[1]), jnp.bfloat16), inputs_row], axis=0)
        mixed_in = short_forward(extended, short_filter, offsets).astype(jnp.bfloat16)
        queries = mixed_in[:, :model_width]
        key_part = mixed_in[:, model_width:2 * model_width]
        value_part = mixed_in[:, 2 * model_width:]
        product = (key_part.astype(jnp.float32) * value_part.astype(jnp.float32)).astype(jnp.bfloat16)
        grad_mix = (grad_row.astype(jnp.float32) * queries.astype(jnp.float32)).astype(jnp.bfloat16)
        source = jnp.concatenate([jnp.zeros((tap_count, model_width), jnp.bfloat16), product], axis=0)

        def block_step(state_pair, block_id):
            spread_acc, kernel_grad = state_pair
            first_row = block_id * tap_count
            window = lax.dynamic_slice_in_dim(source, first_row, 2 * tap_count, 0).astype(jnp.float32).reshape(2 * tap_count, groups, -1)
            near_offs = lax.dynamic_slice_in_dim(offsets, first_row, tap_count, 0)
            keep_mask = row_ids + tap_count - col_ids <= near_offs[:, None]
            masked = jnp.where(keep_mask[None], kernel, 0.0)
            grad_block = lax.dynamic_slice_in_dim(grad_mix, first_row, tap_count, 0).astype(jnp.float32).reshape(tap_count, groups, -1)
            mixed_block = jnp.einsum('gis,sgc->igc', masked, window, precision=lax.Precision.HIGHEST)
            spread = jnp.einsum('gis,igc->sgc', masked, grad_block, precision=lax.Precision.HIGHEST)
            inner_prod = jnp.einsum('igc,sgc->gis', grad_block, window, precision=lax.Precision.HIGHEST)
            kernel_grad = kernel_grad + jnp.where(keep_mask[None], inner_prod, 0.0)
            old_part = lax.dynamic_slice_in_dim(spread_acc, first_row, 2 * tap_count, 0)
            spread_acc = lax.dynamic_update_slice_in_dim(spread_acc, old_part + spread.reshape(2 * tap_count, model_width), first_row, 0)
            return ((spread_acc, kernel_grad), mixed_block.reshape(tap_count, model_width))
        init_state = (jnp.zeros((length + tap_count, model_width), jnp.float32), jnp.zeros((groups, tap_count, 2 * tap_count), jnp.float32))
        (spread_acc, kernel_grad), mixed_blocks = lax.scan(block_step, init_state, jnp.arange(blocks, dtype=jnp.int32))
        long_mix = mixed_blocks.reshape(length, model_width).astype(jnp.bfloat16)
        grad_product = spread_acc[tap_count:].astype(jnp.float32).astype(jnp.bfloat16)
        block_out = (queries.astype(jnp.float32) * long_mix.astype(jnp.float32)).astype(jnp.bfloat16)
        grad_queries = (grad_row.astype(jnp.float32) * long_mix.astype(jnp.float32)).astype(jnp.bfloat16)
        grad_keys = (grad_product.astype(jnp.float32) * value_part.astype(jnp.float32)).astype(jnp.bfloat16)
        grad_values = (grad_product.astype(jnp.float32) * key_part.astype(jnp.float32)).astype(jnp.bfloat16)
        mixed_grad = jnp.concatenate([grad_queries, grad_keys, grad_values], axis=1)
        grads_ext = jnp.concatenate([mixed_grad, jnp.zeros((short_taps - 1, mixed_grad.shape[1]), jnp.bfloat16)], axis=0)
        offsets_ext = jnp.concatenate([offsets, jnp.zeros((short_taps - 1,), jnp.int32)], axis=0)
        grad_inputs, weight_grad = short_backward(grads_ext, offsets_ext, extended, short_filter, offsets)
        return (block_out, grad_inputs.astype(jnp.bfloat16), weight_grad, kernel_grad)
    block_out, grad_projected, weight_grads, kernel_grads = lax.map(one_window, (projected, doc_ids, cotangent))
    norm_scale = N_DP * length
    grad_short = lax.optimization_barrier(jnp.sum(weight_grads, axis=0)) / math.sqrt(norm_scale)
    _, pull_back = jax.vjp(toeplitz, long_filter.astype(jnp.float32))
    group_size = model_width // groups
    grad_long = pull_back(lax.optimization_barrier(jnp.sum(kernel_grads, axis=0)))[0] / math.sqrt(norm_scale * group_size)
    return (block_out, grad_projected, grad_short, grad_long)
```

```python
import math

import jax
import jax.numpy as jnp
from jax import lax
from jax.experimental import pallas as pl
from jax.experimental.pallas import tpu as pltpu
from jax.sharding import PartitionSpec as P

BF = jnp.bfloat16
F32 = jnp.float32
LANES = 128
EDGE = 16
VMEM = 48 * 1024 * 1024


def passed_along(value, axis, steps):
    count = lax.axis_size(axis)
    initial, last = (max(0, -steps), min(count, count - steps))
    return lax.ppermute(value, axis, [(source, source + steps) for source in range(initial, last)])


def swapped(value, axis, bits):
    count = lax.axis_size(axis)
    return lax.ppermute(value, axis, [(source, source ^ bits) for source in range(count)])


def whole(shape):
    return pl.BlockSpec(shape, lambda *_: (0,) * len(shape))


def call(kernel, name, grid, in_specs, out_specs, out_shape, cost, scratch=()):
    return pl.pallas_call(
        kernel,
        name=name,
        grid=grid,
        in_specs=in_specs,
        out_specs=out_specs,
        out_shape=out_shape,
        scratch_shapes=list(scratch),
        compiler_params=pltpu.CompilerParams(vmem_limit_bytes=VMEM),
        cost_estimate=pl.CostEstimate(flops=cost[0], bytes_accessed=cost[1], transcendentals=0),
    )


def mask_kernel(ids_ref, long_ref, back_ref, ahead_ref):
    taps = ids_ref.shape[1]
    prev_row, here_row, next_row = [
        jnp.broadcast_to(ids_ref[i : i + 1, :].astype(F32), (taps, taps)) for i in range(3)
    ]
    here_col = jnp.transpose(here_row)
    rows = lax.broadcasted_iota(jnp.int32, (taps, taps), 0)
    cols = lax.broadcasted_iota(jnp.int32, (taps, taps), 1)

    def put(condition):
        return jnp.where(condition, 1.0, 0.0).astype(BF)

    same = here_col == here_row
    long_ref[0] = put((cols <= rows) & same)
    long_ref[1] = put((cols > rows) & (here_col == prev_row))
    long_ref[2] = put((cols >= rows) & same)
    long_ref[3] = put((cols < rows) & (here_col == next_row))
    last_prev = here_col == pltpu.roll(prev_row, 2, 1)
    first_next = here_col == next_row
    for j in (1, 2):
        at = slice((j - 1) * taps, j * taps)
        back_ref[at, :taps] = put((cols == rows - j) & same)
        back_ref[at, taps:] = put((cols < 2) & (cols == rows + 2 - j) & last_prev)[:, :EDGE]
        ahead_ref[at, :taps] = put((cols == rows + j) & same)
        ahead_ref[at, taps:] = put((cols < 2) & (cols == rows + j - taps) & first_next)[:, :EDGE]


def make_masks(ids3):
    taps = ids3.shape[1]
    return call(
        mask_kernel,
        "masks",
        (),
        [whole(ids3.shape)],
        [whole((4, taps, taps)), whole((2 * taps, taps + EDGE)), whole((2 * taps, taps + EDGE))],
        [
            jax.ShapeDtypeStruct((4, taps, taps), BF),
            jax.ShapeDtypeStruct((2 * taps, taps + EDGE), BF),
            jax.ShapeDtypeStruct((2 * taps, taps + EDGE), BF),
        ],
        (100000, 400000),
    )(ids3)


def turn_kernel(filter_ref, out_ref):
    group_step, taps = filter_ref.shape
    values = filter_ref[...].astype(F32)
    for g in range(group_step):
        spread = jnp.broadcast_to(values[g : g + 1], (taps, taps))
        out_ref[g] = pltpu.roll(spread, 0, 1, stride=1, stride_axis=0).astype(BF)


def make_turned(filters):
    groups, taps = filters.shape
    group_step = 32
    return call(
        turn_kernel,
        "circulants",
        (groups // group_step,),
        [pl.BlockSpec((group_step, taps), lambda i: (i, 0))],
        pl.BlockSpec((group_step, taps, taps), lambda i: (i, 0, 0)),
        jax.ShapeDtypeStruct((groups, taps, taps), BF),
        (groups * taps * taps * 40, groups * taps * taps * 2),
    )(filters)


def extended(values, edge):
    blank = jnp.zeros((EDGE - edge.shape[0], edge.shape[1]), BF)
    return jnp.concatenate([values, edge, blank], axis=0)


def shifted(mask_ref, values, edge):
    taps = values.shape[0]
    both = jnp.dot(mask_ref[...], extended(values, edge), preferred_element_type=F32)
    return both[:taps], both[taps:]


def short_sum(weights, values, one, two):
    return (weights[0:1] * values.astype(F32) + weights[1:2] * one) + weights[2:3] * two


def gate_kernel(
    xq, xk, xv, eq, ek, ev, wq, wk, wv, cot_ref, mask_ref, mixed_ref, product_ref, grad_ref
):
    mixed = []
    for x_ref, e_ref, w_ref in ((xq, eq, wq), (xk, ek, wk), (xv, ev, wv)):
        values = x_ref[...]
        one, two = shifted(mask_ref, values, e_ref[...])
        mixed.append(short_sum(w_ref[...], values, one, two).astype(BF))
    for i in range(3):
        mixed_ref[i] = mixed[i]
    product_ref[...] = mixed[1] * mixed[2]
    grad_ref[...] = cot_ref[...] * mixed[0]


def branch_specs(rows, width, steps):
    return [pl.BlockSpec((rows, width), lambda i, b=b: (0, i + b * steps)) for b in range(3)]


def make_gates(inputs, border, weights, cotangent, back_mask):
    rows, model_width = cotangent.shape
    width = 512
    steps = model_width // width
    plain = pl.BlockSpec((rows, width), lambda i: (0, i))
    return call(
        gate_kernel,
        "gates",
        (steps,),
        branch_specs(rows, width, steps)
        + branch_specs(border.shape[0], width, steps)
        + branch_specs(weights.shape[0], width, steps)
        + [plain, whole(back_mask.shape)],
        [pl.BlockSpec((3, rows, width), lambda i: (0, 0, i)), plain, plain],
        [
            jax.ShapeDtypeStruct((3, rows, model_width), BF),
            jax.ShapeDtypeStruct((rows, model_width), BF),
            jax.ShapeDtypeStruct((rows, model_width), BF),
        ],
        (2 * 256 * 144 * 3 * model_width, 9 * rows * model_width * 2),
    )(inputs, inputs, inputs, border, border, border, weights, weights, weights, cotangent, back_mask)


def long_kernel(
    here_ref, prev_ref, grad_ref, next_ref, fwd_ref, bwd_ref, long_ref, back_ref,
    mixed_ref, cot_ref, xq, xk, xv, eq, ek, ev,
    out_ref, mg_ref, gl_ref, gs_ref, diag,
):
    taps = here_ref.shape[0]
    subs = here_ref.shape[1] // LANES
    per = fwd_ref.shape[0] // subs
    share = LANES // per
    lane_group = lax.broadcasted_iota(jnp.int32, (1, LANES), 1) // share
    lane = [jnp.where(lane_group == g, 1.0, 0.0).astype(BF) for g in range(per)]
    rows = lax.broadcasted_iota(jnp.int32, (8, taps), 0)
    cols = lax.broadcasted_iota(jnp.int32, (8, taps), 1)
    keep = (long_ref[2] + long_ref[3]).astype(F32)

    def long_conv(turned, first, second, stacked):
        left = jnp.concatenate(
            [turned[g] * mask for g in range(per) for mask in (first, second)], axis=1
        )
        right = jnp.concatenate([stacked * lane[g] for g in range(per)], axis=0)
        return jnp.dot(left, right, preferred_element_type=F32)

    for u in range(subs):
        ls = slice(u * LANES, (u + 1) * LANES)
        gs = slice(u * per, (u + 1) * per)
        here, grad = here_ref[:, ls], grad_ref[:, ls]
        sources = jnp.concatenate([here, prev_ref[:, ls]], axis=0)
        grads = jnp.concatenate([grad, next_ref[:, ls]], axis=0)
        long_mix = long_conv(fwd_ref[gs], long_ref[0], long_ref[1], sources).astype(BF)
        grad_product = long_conv(bwd_ref[gs], long_ref[2], long_ref[3], grads).astype(BF)
        out_ref[:, ls] = mixed_ref[0, :, ls] * long_mix
        mg_ref[0, :, ls] = cot_ref[:, ls] * long_mix
        mg_ref[1, :, ls] = grad_product * mixed_ref[2, :, ls]
        mg_ref[2, :, ls] = grad_product * mixed_ref[1, :, ls]

        spread = jnp.concatenate([here * lane[g] for g in range(per)], axis=0)
        inner = lax.dot_general(
            spread, grads, (((1,), (1,)), ((), ())), preferred_element_type=F32
        ).reshape(per, taps // 8, 8, 2 * taps)
        total = None
        for k in range(taps // 8):
            nearer = (cols >= rows + 8 * k)[None]
            term = jnp.where(nearer, inner[:, k, :, :taps], inner[:, k, :, taps:])
            term = (term * keep[8 * k : 8 * k + 8][None]).reshape(per * 8, taps)
            if k:
                term = pltpu.roll(term, taps - 8 * k, 1)
            total = term if total is None else total + term
        diag[u] = total.reshape(per, 8, taps)
        lined = diag[u, :, 0, :]
        for r in range(1, 8):
            lined = lined + pltpu.roll(diag[u, :, r, :], taps - r, 1)
        gl_ref[gs, :] = lined

    for b, (x_ref, e_ref) in enumerate(((xq, eq), (xk, ek), (xv, ev))):
        values = x_ref[...]
        one, two = shifted(back_ref, values, e_ref[...])
        local_grad = mg_ref[b].astype(F32)
        for j, part in enumerate((values.astype(F32), one, two)):
            summed = jnp.sum(local_grad * part, axis=0, keepdims=True)
            for u in range(subs):
                gs_ref[b, 0, j * subs + u : j * subs + u + 1, :] = summed[
                    :, u * LANES : (u + 1) * LANES
                ]


def make_long(product, before, grad_mix, after, fwd, bwd, long_masks, back_mask, mixed, cotangent,
              inputs, border):
    rows, model_width = product.shape
    groups, taps, _ = fwd.shape
    width = 512
    steps = model_width // width
    subs = width // LANES
    step_groups = groups // steps
    plain = pl.BlockSpec((rows, width), lambda i: (0, i))
    tiles = pl.BlockSpec((step_groups, taps, taps), lambda i: (i, 0, 0))
    triple = pl.BlockSpec((3, rows, width), lambda i: (0, 0, i))
    return call(
        long_kernel,
        "long_parts",
        (steps,),
        [plain] * 4
        + [tiles] * 2
        + [whole(long_masks.shape), whole(back_mask.shape), triple, plain]
        + branch_specs(rows, width, steps)
        + branch_specs(border.shape[0], width, steps),
        [
            plain,
            triple,
            pl.BlockSpec((step_groups, taps), lambda i: (i, 0)),
            pl.BlockSpec((3, 1, 3 * subs, LANES), lambda i: (0, i, 0, 0)),
        ],
        [
            jax.ShapeDtypeStruct((rows, model_width), BF),
            jax.ShapeDtypeStruct((3, rows, model_width), BF),
            jax.ShapeDtypeStruct((groups, taps), F32),
            jax.ShapeDtypeStruct((3, steps, 3 * subs, LANES), F32),
        ],
        (3 * groups * 2 * 128 * 256 * 256, 40 * 1024 * 1024),
        [pltpu.VMEM((subs, step_groups // subs, 8, taps), F32)],
    )(product, before, grad_mix, after, fwd, bwd, long_masks, back_mask, mixed, cotangent,
      inputs, inputs, inputs, border, border, border)


def input_grad_kernel(mg_ref, edge_ref, w_ref, mask_ref, out_ref):
    values = mg_ref[0]
    one, two = shifted(mask_ref, values, edge_ref[0])
    out_ref[...] = short_sum(w_ref[...], values, one, two).astype(BF)


def make_input_grad(mixed_grad, edge, weights, ahead_mask):
    _, rows, model_width = mixed_grad.shape
    width = 1024
    steps = model_width // width
    return call(
        input_grad_kernel,
        "input_grads",
        (3, steps),
        [
            pl.BlockSpec((1, rows, width), lambda b, i: (b, 0, i)),
            pl.BlockSpec((1, edge.shape[1], width), lambda b, i: (b, 0, i)),
            pl.BlockSpec((weights.shape[0], width), lambda b, i: (0, b * steps + i)),
            whole(ahead_mask.shape),
        ],
        pl.BlockSpec((rows, width), lambda b, i: (0, b * steps + i)),
        jax.ShapeDtypeStruct((rows, 3 * model_width), BF),
        (2 * 256 * 144 * 3 * model_width, 6 * rows * model_width * 2),
    )(mixed_grad, edge, weights, ahead_mask)


def summed_over_windows(value):
    count = lax.axis_size("dp")
    if count & (count - 1):
        return lax.psum(value, "dp")
    parts = [value] + [swapped(value, "dp", bits) for bits in range(1, count)]
    while len(parts) > 1:
        parts = [parts[i] + parts[i + 1] for i in range(0, len(parts), 2)]
    return parts[0]


def owned_sums(short_parts, long_parts):
    branches, steps, short_rows, lanes = short_parts.shape
    groups, taps = long_parts.shape
    subs = short_rows // 3
    ctx_parts = lax.axis_size("ctx")
    pieces = branches * steps
    if ctx_parts != 8 or pieces % ctx_parts or lanes != taps:
        weight_grad = short_parts.reshape(branches, steps, 3, subs, lanes).transpose(2, 0, 1, 3, 4)
        weight_part = lax.psum_scatter(
            weight_grad.reshape(3, -1), "ctx", scatter_dimension=1, tiled=True
        )
        filter_part = lax.psum_scatter(long_parts, "ctx", scatter_dimension=0, tiled=True)
        return lax.psum((weight_part, filter_part), "dp")
    held = pieces // ctx_parts
    short_owned = short_parts.reshape(ctx_parts, held * short_rows, lanes)
    long_owned = long_parts.reshape(ctx_parts, groups // ctx_parts, taps)
    joined = jnp.concatenate([short_owned, long_owned], axis=1)
    height = joined.shape[1]
    my_index = lax.axis_index("ctx")
    core, chip = my_index % 2, my_index // 2
    by_core = joined.reshape(ctx_parts // 2, 2, height, lanes)
    kept = lax.dynamic_index_in_dim(by_core, core, 1, keepdims=False)
    given = lax.dynamic_index_in_dim(by_core, 1 - core, 1, keepdims=False)
    paired = kept + swapped(given, "ctx", 1)
    mine = lax.dynamic_index_in_dim(paired, chip, 0, keepdims=False)
    others = [
        swapped(lax.dynamic_index_in_dim(paired, chip ^ d, 0, keepdims=False), "ctx", 2 * d)
        for d in range(1, ctx_parts // 2)
    ]
    total = (mine + others[0]) + (others[1] + others[2])
    total = summed_over_windows(total)
    short_total = total[: held * short_rows].reshape(held, 3, subs, lanes).transpose(1, 0, 2, 3)
    return short_total.reshape(3, held * subs * lanes), total[held * short_rows :]


def local(projected, doc_ids, short_filter, long_filter, cotangent):
    inputs_row = projected[0]
    grad_row = cotangent[0]
    seg_row = doc_ids[0]
    rows, model_width = grad_row.shape
    groups, taps = long_filter.shape
    short_taps = short_filter.shape[0]
    length = seg_row.shape[0]
    my_index = lax.axis_index("ctx")
    edge = short_taps - 1
    border = passed_along(inputs_row[rows - edge :], "ctx", 1)
    blank = jnp.full((rows,), -1, jnp.int32)
    ids_pad = jnp.concatenate([blank, seg_row, blank])
    ids3 = lax.dynamic_slice_in_dim(ids_pad, my_index * rows, 3 * rows, 0).reshape(3, rows)
    long_masks, back_mask, ahead_mask = make_masks(ids3)
    fwd = make_turned(jnp.roll(long_filter[:, ::-1], 1, axis=1))
    mixed, product, grad_mix = make_gates(inputs_row, border, short_filter, grad_row, back_mask)
    before = passed_along(product, "ctx", 1)
    after = passed_along(grad_mix, "ctx", -1)
    bwd = make_turned(long_filter)
    block_out, mixed_grad, long_parts, short_parts = make_long(
        product, before, grad_mix, after, fwd, bwd, long_masks, back_mask, mixed, grad_row,
        inputs_row, border,
    )
    ahead_rows = passed_along(mixed_grad[:, :edge], "ctx", -1)
    grad_inputs = make_input_grad(mixed_grad, ahead_rows, short_filter, ahead_mask)
    weight_total, filter_total = owned_sums(short_parts, long_parts)
    norm_scale = lax.axis_size("dp") * length
    group_size = model_width // groups
    grad_short = weight_total / math.sqrt(norm_scale)
    grad_long = filter_total / math.sqrt(norm_scale * group_size)
    return (block_out[None], grad_inputs[None], grad_short, grad_long)


def solution(mesh):
    return jax.shard_map(
        local,
        mesh=mesh,
        in_specs=(P("dp", "ctx", None), P("dp", None), P(), P(), P("dp", "ctx", None)),
        out_specs=(P("dp", "ctx", None), P("dp", "ctx", None), P(None, "ctx"), P("ctx", None)),
        check_vma=False,
    )
```

```python
import functools
import math

import jax
import jax.numpy as jnp
from jax import lax
from jax.experimental import pallas as pl
from jax.experimental.pallas import tpu as pltpu
from jax.sharding import PartitionSpec as P

BF = jnp.bfloat16
F32 = jnp.float32
LANES = 128
EDGE = 16
WIDTH = 512
PARTS = 2
VMEM = 32 * 1024 * 1024


def passed_along(value, axis, steps):
    count = lax.axis_size(axis)
    initial, last = (max(0, -steps), min(count, count - steps))
    return lax.ppermute(value, axis, [(source, source + steps) for source in range(initial, last)])


def swapped(value, axis, bits):
    count = lax.axis_size(axis)
    return lax.ppermute(value, axis, [(source, source ^ bits) for source in range(count)])


def linked(value, axis):
    count = lax.axis_size(axis)
    pairs = [(i, i + 1) for i in range(1, count - 1, 2)]
    return lax.ppermute(value, axis, pairs + [(b, a) for a, b in pairs])


def whole(shape):
    return pl.BlockSpec(shape, lambda *_: (0,) * len(shape))


def call(kernel, name, grid, in_specs, out_specs, out_shape, cost, scratch=(), aliases=None):
    return pl.pallas_call(
        kernel,
        name=name,
        grid=grid,
        in_specs=in_specs,
        out_specs=out_specs,
        out_shape=out_shape,
        scratch_shapes=list(scratch),
        input_output_aliases=aliases or {},
        compiler_params=pltpu.CompilerParams(vmem_limit_bytes=VMEM),
        cost_estimate=pl.CostEstimate(flops=cost[0], bytes_accessed=cost[1], transcendentals=0),
    )


def in_hbm(value):
    return pltpu.with_memory_space_constraint(value, pltpu.HBM)


def prepare_kernel(
    ids_ref, long_ref, back_ref, ahead_ref, late_ref
):
    taps = long_ref.shape[1]
    here = lax.axis_index("ctx")
    last = ids_ref.shape[1] // taps - 1

    def id_row(block, present):
        held = jnp.clip(block, 0, last) * taps
        row = ids_ref[:, pl.ds(pl.multiple_of(held, taps), taps)].astype(F32)
        return jnp.broadcast_to(jnp.where(present, row, -1.0), (taps, taps))

    prev_row = id_row(here - 1, here > 0)
    here_row = id_row(here, here >= 0)
    next_row = id_row(here + 1, here < last)
    here_col = jnp.transpose(here_row)
    rows = lax.broadcasted_iota(jnp.int32, (taps, taps), 0)
    cols = lax.broadcasted_iota(jnp.int32, (taps, taps), 1)

    def put(condition):
        return jnp.where(condition, 1.0, 0.0).astype(BF)

    same = here_col == here_row
    long_ref[0] = put((cols <= rows) & same)
    long_ref[1] = put((cols > rows) & (here_col == prev_row))
    long_ref[2] = put((cols >= rows) & same)
    long_ref[3] = put((cols < rows) & (here_col == next_row))
    long_ref[4] = put(((cols >= rows) & same) | ((cols < rows) & (here_col == next_row)))
    last_prev = here_col == pltpu.roll(prev_row, 2, 1)
    first_next = here_col == next_row
    for j in (1, 2):
        at = slice((j - 1) * taps, j * taps)
        back_ref[at, :taps] = put((cols == rows - j) & same)
        back_ref[at, taps:] = put((cols < 2) & (cols == rows + 2 - j) & last_prev)[:, :EDGE]
        ahead_ref[at, :] = put((cols == rows + j) & same)
        late = jnp.where((cols == rows + j - taps) & first_next, 1.0, 0.0)
        late_ref[j - 1] = late[taps - 8 :]


def prepare(doc_ids, taps):
    shapes = [
        ((5, taps, taps), BF),
        ((2 * taps, taps + EDGE), BF),
        ((2 * taps, taps), BF),
        ((2, 8, taps), F32),
    ]
    return call(
        prepare_kernel,
        "prepare",
        (),
        [whole(doc_ids.shape)],
        [whole(shape) for shape, _ in shapes],
        [jax.ShapeDtypeStruct(*entry) for entry in shapes],
        (1000000, 1000000),
    )(in_hbm(doc_ids))


def short_sum(weights, values, one, two):
    return (weights[0:1] * values.astype(F32) + weights[1:2] * one) + weights[2:3] * two


def gate_kernel(xq, xk, xv, edge_ref, w_ref, cot_ref, mask_ref, mixed_ref, chip_ref, link_ref,
                *, first, steps):
    rows, width = cot_ref.shape
    step = pl.program_id(0) + first
    mixed = []
    for b, x_ref in enumerate((xq, xk, xv)):
        values = x_ref[...]
        at = pl.ds(pl.multiple_of((step + b * steps) * width, width), width)
        edge = edge_ref[:, at]
        blank = jnp.zeros((EDGE - edge.shape[0], width), BF)
        both = jnp.dot(
            mask_ref[...],
            jnp.concatenate([values, edge, blank], axis=0),
            preferred_element_type=F32,
        )
        mixed.append(short_sum(w_ref[:, at], values, both[:rows], both[rows:]).astype(BF))
    for b in range(3):
        mixed_ref[b] = mixed[b]
    product = mixed[1] * mixed[2]
    grad_mix = cot_ref[...] * mixed[0]
    first_core = lax.axis_index("ctx") % 2 == 0
    chip_ref[...] = jnp.where(first_core, product, grad_mix)
    link_ref[...] = jnp.where(first_core, grad_mix, product)


def branch_specs(rows, width, first, steps):
    return [
        pl.BlockSpec((rows, width), lambda i, b=b: (0, first + i + b * steps)) for b in range(3)
    ]


def make_gates(inputs, border, weights, cotangent, back_mask, part, parts):
    rows, model_width = cotangent.shape
    width = WIDTH
    steps = model_width // width
    held = steps // parts
    first = part * held
    plain = pl.BlockSpec((rows, width), lambda i: (0, i))
    return call(
        functools.partial(gate_kernel, first=first, steps=steps),
        "gates",
        (held,),
        branch_specs(rows, width, first, steps)
        + [
            whole(border.shape),
            whole(weights.shape),
            pl.BlockSpec((rows, width), lambda i: (0, first + i)),
            whole(back_mask.shape),
        ],
        [pl.BlockSpec((3, rows, width), lambda i: (0, 0, i)), plain, plain],
        [
            pltpu.VMEM((3, rows, held * width), BF),
            pltpu.VMEM((rows, held * width), BF),
            pltpu.VMEM((rows, held * width), BF),
        ],
        (2 * 256 * 256 * 3 * held * width, 9 * rows * held * width * 2),
    )(inputs, inputs, inputs, border, weights, cotangent, back_mask)


def long_kernel(
    chip_ref, chip_in_ref, link_ref, link_in_ref, filter_ref, long_ref, back_ref, ahead_ref,
    mixed_ref, cot_ref, xq, xk, xv, edge_ref, w_ref, *rest, first, steps, held,
):
    out_ref, head_ref, tail_ref, gl_ref, gs_ref, inputs_ref, diag, staged, sems = rest[-9:]
    rows_here, width = chip_ref.shape
    first_core = lax.axis_index("ctx") % 2 == 0
    taps = filter_ref.shape[1]
    subs = width // LANES
    per = filter_ref.shape[0] // subs
    share = LANES // per
    i = pl.program_id(0)
    slot = lax.rem(i, 2)
    lane_group = lax.broadcasted_iota(jnp.int32, (1, LANES), 1) // share
    lane = [jnp.where(lane_group == g, 1.0, 0.0).astype(BF) for g in range(per)]
    rows = lax.broadcasted_iota(jnp.int32, (8, taps), 0)
    cols = lax.broadcasted_iota(jnp.int32, (8, taps), 1)

    def column(step, b):
        return pl.ds(pl.multiple_of((step + first + b * steps) * width, width), width)

    def leaving(step, b):
        at = lax.rem(step, 2)
        return pltpu.make_async_copy(
            staged.at[at, b], inputs_ref.at[:, column(step, b)], sems.at[at, b]
        )

    @pl.when(i >= 2)
    def _():
        for b in range(3):
            leaving(i - 2, b).wait()

    mixed_grads = [[], [], []]
    for u in range(subs):
        ls = slice(u * LANES, (u + 1) * LANES)
        gs = slice(u * per, (u + 1) * per)
        one_side = jnp.concatenate([chip_ref[:, ls], link_in_ref[:, ls]], axis=0)
        other_side = jnp.concatenate([link_ref[:, ls], chip_in_ref[:, ls]], axis=0)
        sources = jnp.where(first_core, one_side, other_side)
        grads = jnp.where(first_core, other_side, one_side)
        here = sources[:rows_here]
        filters = filter_ref[gs].astype(F32)
        turned = [
            pltpu.roll(
                jnp.broadcast_to(filters[g : g + 1], (taps, taps)), 0, 1, stride=1, stride_axis=0
            ).astype(BF)
            for g in range(per)
        ]
        upright = [jnp.transpose(turned[g]) for g in range(per)]

        def long_conv(circulants, first_mask, stacked):
            left = jnp.concatenate(
                [part * long_ref[first_mask + n] for part in circulants for n in range(2)], axis=1
            )
            right = jnp.concatenate([stacked * lane[g] for g in range(per)], axis=0)
            return jnp.dot(left, right, preferred_element_type=F32).astype(BF)

        long_mix = long_conv(upright, 0, sources)
        grad_product = long_conv(turned, 2, grads)
        out_ref[:, ls] = mixed_ref[0, :, ls] * long_mix
        mixed_grads[0].append(cot_ref[:, ls] * long_mix)
        mixed_grads[1].append(grad_product * mixed_ref[2, :, ls])
        mixed_grads[2].append(grad_product * mixed_ref[1, :, ls])

        spread = jnp.concatenate([here * lane[g] for g in range(per)], axis=0)
        inner = lax.dot_general(
            spread, grads, (((1,), (1,)), ((), ())), preferred_element_type=F32
        ).reshape(per, taps // 8, 8, 2 * taps)
        keep = long_ref[4].astype(F32)
        total = None
        for k in range(taps // 8):
            nearer = (cols >= rows + 8 * k)[None]
            term = jnp.where(nearer, inner[:, k, :, :taps], inner[:, k, :, taps:])
            term = (term * keep[8 * k : 8 * k + 8][None]).reshape(per * 8, taps)
            if k:
                term = pltpu.roll(term, taps - 8 * k, 1)
            total = term if total is None else total + term
        diag[u] = total.reshape(per, 8, taps)
        lined = diag[u, :, 0, :]
        for r in range(1, 8):
            lined = lined + pltpu.roll(diag[u, :, r, :], taps - r, 1)
        gl_ref[gs, :] = lined

    edge_keep = back_ref[:, taps : taps + 2].astype(F32)
    for b, x_ref in enumerate((xq, xk, xv)):
        mixed_grad = jnp.concatenate(mixed_grads[b], axis=1)
        head_ref[b] = mixed_grad[:2]
        both = jnp.dot(ahead_ref[...], mixed_grad, preferred_element_type=F32)
        one, two = both[:rows_here], both[rows_here:]
        at = column(i, b)
        total = short_sum(w_ref[:, at], mixed_grad, one, two)
        tail_ref[b] = total[rows_here - 8 :]
        staged[slot, b] = total.astype(BF)
        leaving(i, b).start()
        values = x_ref[...].astype(F32)
        edge = edge_ref[:, at].astype(F32)
        first_rows = mixed_grad[:16].astype(F32)
        over_edge = (
            None,
            edge_keep[0:1, 1:2] * first_rows[0:1] * edge[1:2],
            edge_keep[taps : taps + 1, 0:1] * first_rows[0:1] * edge[0:1]
            + edge_keep[taps + 1 : taps + 2, 1:2] * first_rows[1:2] * edge[1:2],
        )
        for j, part in enumerate((mixed_grad.astype(F32), one, two)):
            summed = jnp.sum(values * part, axis=0, keepdims=True)
            if j:
                summed = summed + over_edge[j]
            for u in range(subs):
                gs_ref[b, 0, j * subs + u : j * subs + u + 1, :] = summed[
                    :, u * LANES : (u + 1) * LANES
                ]

    @pl.when(i == held - 1)
    def _():
        for b in range(3):
            if held > 1:
                leaving(i - 1, b).wait()
            leaving(i, b).wait()


def make_long(chip, chip_in, link, link_in, filters, masks, mixed, cotangent, inputs, border,
              weights, part, parts, so_far):
    rows, model_width = cotangent.shape
    groups, taps = filters.shape
    width = WIDTH
    steps = model_width // width
    held = steps // parts
    first = part * held
    subs = width // LANES
    step_groups = groups // steps
    long_masks, back_mask, ahead_mask, _ = masks
    plain = pl.BlockSpec((rows, width), lambda i: (0, i))
    placed = pl.BlockSpec((rows, width), lambda i: (0, first + i))
    anywhere = pl.BlockSpec(memory_space=pl.ANY)
    operands = [chip, chip_in, link, link_in, filters, long_masks, back_mask, ahead_mask, mixed,
                cotangent, inputs, inputs, inputs, border, weights]
    in_specs = (
        [plain] * 4
        + [pl.BlockSpec((step_groups, taps), lambda i: (first + i, 0))]
        + [whole(mask.shape) for mask in (long_masks, back_mask, ahead_mask)]
        + [pl.BlockSpec((3, rows, width), lambda i: (0, 0, i)), placed]
        + branch_specs(rows, width, first, steps)
        + [whole(border.shape), whole(weights.shape)]
    )
    aliases = {}
    if so_far is not None:
        aliases = {len(operands) + n: n for n in range(len(so_far))}
        operands = operands + list(so_far)
        in_specs = in_specs + [anywhere] * len(so_far)
    return call(
        functools.partial(long_kernel, first=first, steps=steps, held=held),
        "long_parts",
        (held,),
        in_specs,
        [
            placed,
            pl.BlockSpec((3, 2, width), lambda i: (0, 0, first + i)),
            pl.BlockSpec((3, 8, width), lambda i: (0, 0, first + i)),
            pl.BlockSpec((step_groups, taps), lambda i: (first + i, 0)),
            pl.BlockSpec((3, 1, 3 * subs, LANES), lambda i: (0, first + i, 0, 0)),
            anywhere,
        ],
        [
            jax.ShapeDtypeStruct((rows, model_width), BF),
            jax.ShapeDtypeStruct((3, 2, model_width), BF),
            jax.ShapeDtypeStruct((3, 8, model_width), F32),
            jax.ShapeDtypeStruct((groups, taps), F32),
            jax.ShapeDtypeStruct((3, steps, 3 * subs, LANES), F32),
            jax.ShapeDtypeStruct((rows, 3 * model_width), BF),
        ],
        (3 * groups * 2 * 128 * 256 * 256 // parts, 24 * 1024 * 1024 // parts),
        [
            pltpu.VMEM((subs, step_groups // subs, 8, taps), F32),
            pltpu.VMEM((2, 3, rows, width), BF),
            pltpu.SemaphoreType.DMA((2, 3)),
        ],
        aliases,
    )(*operands)


def last_rows_kernel(tail_ref, ahead_ref, w_ref, late_ref, old_ref, out_ref):
    lines = old_ref.shape[0]
    width = tail_ref.shape[2]
    first_keep, second_keep = late_ref[0, :, 0:1], late_ref[1, :, 0:1]
    next_keep = late_ref[1, :, 1:2]
    for b in range(3):
        at = slice(b * width, (b + 1) * width)
        ahead = ahead_ref[b].astype(F32)
        first, second = ahead[0:1], ahead[1:2]
        extra = w_ref[1:2, at] * (first_keep * first)
        extra = extra + w_ref[2:3, at] * (second_keep * first + next_keep * second)
        ending = (tail_ref[b] + extra).astype(BF)
        out_ref[:, at] = jnp.concatenate([old_ref[: lines // 2, at], ending], axis=0)


def finish_last_rows(grad_inputs, tail, ahead_rows, weights, late_mask):
    rows, total_width = grad_inputs.shape
    lines = 16
    held = pl.BlockSpec((lines, total_width), lambda i: (rows // lines - 1, 0))
    return call(
        last_rows_kernel,
        "last_rows",
        (1,),
        [whole(value.shape) for value in (tail, ahead_rows, weights, late_mask)] + [held],
        held,
        jax.ShapeDtypeStruct(grad_inputs.shape, BF),
        (1000000, 2000000),
        aliases={4: 0},
    )(tail, ahead_rows, weights, late_mask, grad_inputs)


def summed_over_windows(value):
    count = lax.axis_size("dp")
    if count & (count - 1):
        return lax.psum(value, "dp")
    parts = [value] + [swapped(value, "dp", bits) for bits in range(1, count)]
    while len(parts) > 1:
        parts = [parts[i] + parts[i + 1] for i in range(0, len(parts), 2)]
    return parts[0]


def owned_sums(short_parts, long_parts):
    branches, steps, short_rows, lanes = short_parts.shape
    groups, taps = long_parts.shape
    subs = short_rows // 3
    ctx_parts = lax.axis_size("ctx")
    pieces = branches * steps
    if ctx_parts != 8 or pieces % ctx_parts or lanes != taps:
        weight_grad = short_parts.reshape(branches, steps, 3, subs, lanes).transpose(2, 0, 1, 3, 4)
        weight_part = lax.psum_scatter(
            weight_grad.reshape(3, -1), "ctx", scatter_dimension=1, tiled=True
        )
        filter_part = lax.psum_scatter(long_parts, "ctx", scatter_dimension=0, tiled=True)
        return lax.psum((weight_part, filter_part), "dp")
    held = pieces // ctx_parts
    short_owned = short_parts.reshape(ctx_parts, held * short_rows, lanes)
    long_owned = long_parts.reshape(ctx_parts, groups // ctx_parts, taps)
    joined = jnp.concatenate([short_owned, long_owned], axis=1)
    height = joined.shape[1]
    my_index = lax.axis_index("ctx")
    core, chip = my_index % 2, my_index // 2
    by_core = joined.reshape(ctx_parts // 2, 2, height, lanes)
    kept = lax.dynamic_index_in_dim(by_core, core, 1, keepdims=False)
    given = lax.dynamic_index_in_dim(by_core, 1 - core, 1, keepdims=False)
    paired = kept + swapped(given, "ctx", 1)
    mine = lax.dynamic_index_in_dim(paired, chip, 0, keepdims=False)
    others = [
        swapped(lax.dynamic_index_in_dim(paired, chip ^ d, 0, keepdims=False), "ctx", 2 * d)
        for d in range(1, ctx_parts // 2)
    ]
    total = (mine + others[0]) + (others[1] + others[2])
    total = summed_over_windows(total)
    short_total = total[: held * short_rows].reshape(held, 3, subs, lanes).transpose(1, 0, 2, 3)
    return short_total.reshape(3, held * subs * lanes), total[held * short_rows :]


def local(projected, doc_ids, short_filter, long_filter, cotangent):
    grad_row = cotangent[0]
    seg_row = doc_ids[0]
    rows, model_width = grad_row.shape
    groups = long_filter.shape[0]
    short_taps = short_filter.shape[0]
    length = seg_row.shape[0]
    edge = short_taps - 1
    border = passed_along(projected[0, rows - edge :], "ctx", 1)
    filters = in_hbm(long_filter)
    masks = prepare(doc_ids, long_filter.shape[1])
    inputs_row, grad_row, short_filter = [
        in_hbm(value) for value in (projected[0], grad_row, short_filter)
    ]
    gated = []
    for part in range(PARTS):
        mixed, chip, link = make_gates(
            inputs_row, border, short_filter, grad_row, masks[1], part, PARTS
        )
        chip_in = swapped(chip, "ctx", 1)
        link_in = linked(link, "ctx")
        gated.append((mixed, chip, chip_in, link, link_in))
    done = None
    for part, (mixed, chip, chip_in, link, link_in) in enumerate(gated):
        done = make_long(
            chip, chip_in, link, link_in, filters, masks, mixed, grad_row, inputs_row, border,
            short_filter, part, PARTS, done,
        )
    block_out, head, tail, long_parts, short_parts, grad_inputs = done
    ahead_rows = passed_along(head, "ctx", -1)
    grad_inputs = finish_last_rows(grad_inputs, tail, ahead_rows, short_filter, masks[3])
    weight_total, filter_total = owned_sums(short_parts, long_parts)
    norm_scale = lax.axis_size("dp") * length
    group_size = model_width // groups
    grad_short = weight_total / math.sqrt(norm_scale)
    grad_long = filter_total / math.sqrt(norm_scale * group_size)
    return (block_out[None], grad_inputs[None], grad_short, grad_long)


def solution(mesh):
    return jax.shard_map(
        local,
        mesh=mesh,
        in_specs=(P("dp", "ctx", None), P("dp", None), P(), P(), P("dp", "ctx", None)),
        out_specs=(P("dp", "ctx", None), P("dp", "ctx", None), P(None, "ctx"), P("ctx", None)),
        check_vma=False,
    )
```

```python
import functools
import math

import jax
import jax.numpy as jnp
from jax import lax
from jax.experimental import pallas as pl
from jax.experimental.pallas import tpu as pltpu
from jax.sharding import PartitionSpec as P

BF = jnp.bfloat16
F32 = jnp.float32
LANES = 128
EDGE = 16
WIDTH = 1024
GATE_WIDTH = 2048
PIECE = 4
PARTS = 2


def passed_along(value, axis, steps):
    count = lax.axis_size(axis)
    initial, last = (max(0, -steps), min(count, count - steps))
    return lax.ppermute(value, axis, [(source, source + steps) for source in range(initial, last)])


def swapped(value, axis, bits):
    count = lax.axis_size(axis)
    return lax.ppermute(value, axis, [(source, source ^ bits) for source in range(count)])


def linked(value, axis):
    count = lax.axis_size(axis)
    pairs = [(i, i + 1) for i in range(1, count - 1, 2)]
    return lax.ppermute(value, axis, pairs + [(b, a) for a, b in pairs])


def whole(shape):
    return pl.BlockSpec(shape, lambda *_: (0,) * len(shape))


def call(
    kernel, name, grid, in_specs, out_specs, out_shape, cost, scratch=(), aliases=None, mib=16
):
    return pl.pallas_call(
        kernel,
        name=name,
        grid=grid,
        in_specs=in_specs,
        out_specs=out_specs,
        out_shape=out_shape,
        scratch_shapes=list(scratch),
        input_output_aliases=aliases or {},
        compiler_params=pltpu.CompilerParams(vmem_limit_bytes=mib * 1024 * 1024),
        cost_estimate=pl.CostEstimate(flops=cost[0], bytes_accessed=cost[1], transcendentals=0),
    )


def in_hbm(value):
    return pltpu.with_memory_space_constraint(value, pltpu.HBM)


def prepare_kernel(
    ids_ref, long_ref, back_ref, ahead_ref, late_ref
):
    taps = long_ref.shape[1]
    here = lax.axis_index("ctx")
    last = ids_ref.shape[1] // taps - 1

    def id_row(block, present):
        held = jnp.clip(block, 0, last) * taps
        row = ids_ref[:, pl.ds(pl.multiple_of(held, taps), taps)].astype(F32)
        return jnp.broadcast_to(jnp.where(present, row, -1.0), (taps, taps))

    prev_row = id_row(here - 1, here > 0)
    here_row = id_row(here, here >= 0)
    next_row = id_row(here + 1, here < last)
    here_col = jnp.transpose(here_row)
    prev_col = jnp.transpose(prev_row)
    rows = lax.broadcasted_iota(jnp.int32, (taps, taps), 0)
    cols = lax.broadcasted_iota(jnp.int32, (taps, taps), 1)

    def put(condition):
        return jnp.where(condition, 1.0, 0.0).astype(BF)

    same = here_col == here_row
    long_ref[0] = put((cols >= rows) & same)
    long_ref[1] = put((cols < rows) & (prev_col == here_row))
    long_ref[2] = put((cols < rows) & (here_col == next_row))
    long_ref[3] = put(((cols >= rows) & same) | ((cols < rows) & (here_col == next_row)))
    last_prev = here_col == pltpu.roll(prev_row, 2, 1)
    first_next = here_col == next_row
    for j in (1, 2):
        at = slice((j - 1) * taps, j * taps)
        back_ref[at, :taps] = put((cols == rows - j) & same)
        back_ref[at, taps:] = put((cols < 2) & (cols == rows + 2 - j) & last_prev)[:, :EDGE]
        ahead_ref[at, :] = put((cols == rows + j) & same)
        late = jnp.where((cols == rows + j - taps) & first_next, 1.0, 0.0)
        late_ref[j - 1] = late[taps - 8 :]


def prepare(doc_ids, taps):
    shapes = [
        ((4, taps, taps), BF),
        ((2 * taps, taps + EDGE), BF),
        ((2 * taps, taps), BF),
        ((2, 8, taps), F32),
    ]
    return call(
        prepare_kernel,
        "prepare",
        (),
        [whole(doc_ids.shape)],
        [whole(shape) for shape, _ in shapes],
        [jax.ShapeDtypeStruct(*entry) for entry in shapes],
        (1000000, 1000000),
    )(in_hbm(doc_ids))


def short_sum(weights, values, one, two):
    return (weights[0:1] * values.astype(F32) + weights[1:2] * one) + weights[2:3] * two


def gate_kernel(xq, xk, xv, edge_ref, w_ref, cot_ref, mask_ref, mixed_ref, chip_ref, link_ref,
                *, first, steps):
    rows, width = cot_ref.shape
    step = pl.program_id(0) + first
    mixed = []
    for b, x_ref in enumerate((xq, xk, xv)):
        values = x_ref[...]
        at = pl.ds(pl.multiple_of((step + b * steps) * width, width), width)
        edge = edge_ref[:, at]
        blank = jnp.zeros((EDGE - edge.shape[0], width), BF)
        both = jnp.dot(
            mask_ref[...],
            jnp.concatenate([values, edge, blank], axis=0),
            preferred_element_type=F32,
        )
        mixed.append(short_sum(w_ref[:, at], values, both[:rows], both[rows:]).astype(BF))
    for b in range(3):
        mixed_ref[b] = mixed[b]
    product = mixed[1] * mixed[2]
    grad_mix = cot_ref[...] * mixed[0]
    first_core = lax.axis_index("ctx") % 2 == 0
    chip_ref[...] = jnp.where(first_core, product, grad_mix)
    link_ref[...] = jnp.where(first_core, grad_mix, product)


def branch_specs(rows, width, first, steps):
    return [
        pl.BlockSpec((rows, width), lambda i, b=b: (0, first + i + b * steps)) for b in range(3)
    ]


def make_gates(inputs, border, weights, cotangent, back_mask, part, parts):
    rows, model_width = cotangent.shape
    width = GATE_WIDTH
    steps = model_width // width
    held = steps // parts
    first = part * held
    plain = pl.BlockSpec((rows, width), lambda i: (0, i))
    return call(
        functools.partial(gate_kernel, first=first, steps=steps),
        "gates",
        (held,),
        branch_specs(rows, width, first, steps)
        + [
            whole(border.shape),
            whole(weights.shape),
            pl.BlockSpec((rows, width), lambda i: (0, first + i)),
            whole(back_mask.shape),
        ],
        [pl.BlockSpec((3, rows, width), lambda i: (0, 0, i)), plain, plain],
        [
            pltpu.VMEM((3, rows, held * width), BF),
            pltpu.VMEM((rows, held * width), BF),
            pltpu.VMEM((rows, held * width), BF),
        ],
        (2 * 256 * 256 * 3 * held * width, 9 * rows * held * width * 2),
        mib=32,
    )(inputs, inputs, inputs, border, weights, cotangent, back_mask)


def long_kernel(
    chip_in_ref, link_in_ref, filter_ref, long_ref, back_ref, ahead_ref,
    mixed_ref, cot_ref, xq, xk, xv, edge_ref, w_ref, *rest, first, steps, held,
):
    out_ref, head_ref, tail_ref, gl_ref, gs_ref, inputs_ref, diag, staged, sems = rest[-9:]
    rows_here, width = chip_in_ref.shape
    first_core = lax.axis_index("ctx") % 2 == 0
    taps = filter_ref.shape[1]
    subs = width // LANES
    per = filter_ref.shape[0] // subs
    share = LANES // per
    i = pl.program_id(0)
    slot = lax.rem(i, 2)
    lane_group = lax.broadcasted_iota(jnp.int32, (1, LANES), 1) // share
    lane = [jnp.where(lane_group == g, 1.0, 0.0).astype(BF) for g in range(per)]
    rows = lax.broadcasted_iota(jnp.int32, (8, taps), 0)
    cols = lax.broadcasted_iota(jnp.int32, (8, taps), 1)

    def column(step, b):
        return pl.ds(pl.multiple_of((step + first + b * steps) * width, width), width)

    def leaving(step, b):
        at = lax.rem(step, 2)
        return pltpu.make_async_copy(
            staged.at[at, b], inputs_ref.at[:, column(step, b)], sems.at[at, b]
        )

    @pl.when(i >= 2)
    def _():
        for b in range(3):
            leaving(i - 2, b).wait()

    mixed_grads = [[], [], []]
    for u in range(subs):
        ls = slice(u * LANES, (u + 1) * LANES)
        gs = slice(u * per, (u + 1) * per)
        here = mixed_ref[1, :, ls] * mixed_ref[2, :, ls]
        grad = cot_ref[:, ls] * mixed_ref[0, :, ls]
        chip_in, link_in = chip_in_ref[:, ls], link_in_ref[:, ls]
        sources = jnp.concatenate([here, jnp.where(first_core, link_in, chip_in)], axis=0)
        grads = jnp.concatenate([grad, jnp.where(first_core, chip_in, link_in)], axis=0)
        filters = filter_ref[gs].astype(F32)
        turned = [
            pltpu.roll(
                jnp.broadcast_to(filters[g : g + 1], (taps, taps)), 0, 1, stride=1, stride_axis=0
            ).astype(BF)
            for g in range(per)
        ]
        near = [part * long_ref[0] for part in turned]

        def long_conv(far, stacked, dims):
            across = jnp.transpose(stacked)
            parts = []
            for g in range(per):
                taken = across[g * share : (g + 1) * share]
                right = jnp.concatenate([near[g], turned[g] * long_ref[far]], axis=dims)
                parts.append(
                    lax.dot_general(
                        taken, right, (((1,), (dims,)), ((), ())), preferred_element_type=F32
                    )
                )
            return jnp.transpose(jnp.concatenate(parts, axis=0).astype(BF))

        long_mix = long_conv(1, sources, 0)
        grad_product = long_conv(2, grads, 1)
        out_ref[:, ls] = mixed_ref[0, :, ls] * long_mix
        mixed_grads[0].append(cot_ref[:, ls] * long_mix)
        mixed_grads[1].append(grad_product * mixed_ref[2, :, ls])
        mixed_grads[2].append(grad_product * mixed_ref[1, :, ls])

        spread = jnp.concatenate([here * lane[g] for g in range(per)], axis=0)
        inner = lax.dot_general(
            spread, grads, (((1,), (1,)), ((), ())), preferred_element_type=F32
        ).reshape(per, taps // 8, 8, 2 * taps)
        keep = long_ref[3].astype(F32)
        total = None
        for k in range(taps // 8):
            nearer = (cols >= rows + 8 * k)[None]
            term = jnp.where(nearer, inner[:, k, :, :taps], inner[:, k, :, taps:])
            term = (term * keep[8 * k : 8 * k + 8][None]).reshape(per * 8, taps)
            if k:
                term = pltpu.roll(term, taps - 8 * k, 1)
            total = term if total is None else total + term
        diag[u] = total.reshape(per, 8, taps)
        lined = diag[u, :, 0, :]
        for r in range(1, 8):
            lined = lined + pltpu.roll(diag[u, :, r, :], taps - r, 1)
        gl_ref[gs, :] = lined

    edge_keep = back_ref[:, taps : taps + 2].astype(F32)
    for b, x_ref in enumerate((xq, xk, xv)):
        mixed_grad = jnp.concatenate(mixed_grads[b], axis=1)
        first_rows = mixed_grad[:16].astype(F32)
        for u in range(subs):
            for r in range(2):
                at_row = r * PIECE + u % PIECE
                head_ref[b, u // PIECE, at_row : at_row + 1, :] = first_rows[
                    r : r + 1, u * LANES : (u + 1) * LANES
                ]
        both = jnp.dot(ahead_ref[...], mixed_grad, preferred_element_type=F32)
        one, two = both[:rows_here], both[rows_here:]
        at = column(i, b)
        total = short_sum(w_ref[:, at], mixed_grad, one, two)
        tail_ref[b] = total[rows_here - 8 :]
        staged[slot, b] = total.astype(BF)
        leaving(i, b).start()
        values = x_ref[...].astype(F32)
        edge = edge_ref[:, at].astype(F32)
        over_edge = (
            None,
            edge_keep[0:1, 1:2] * first_rows[0:1] * edge[1:2],
            edge_keep[taps : taps + 1, 0:1] * first_rows[0:1] * edge[0:1]
            + edge_keep[taps + 1 : taps + 2, 1:2] * first_rows[1:2] * edge[1:2],
        )
        for j, part in enumerate((mixed_grad.astype(F32), one, two)):
            summed = jnp.sum(values * part, axis=0, keepdims=True)
            if j:
                summed = summed + over_edge[j]
            for u in range(subs):
                at_row = j * PIECE + u % PIECE
                gs_ref[b, u // PIECE, at_row : at_row + 1, :] = summed[
                    :, u * LANES : (u + 1) * LANES
                ]

    @pl.when(i == held - 1)
    def _():
        for b in range(3):
            if held > 1:
                leaving(i - 1, b).wait()
            leaving(i, b).wait()


def make_long(chip_in, link_in, filters, masks, mixed, cotangent, inputs, border,
              weights, part, parts, so_far):
    rows, model_width = cotangent.shape
    groups, taps = filters.shape
    width = WIDTH
    steps = model_width // width
    held = steps // parts
    first = part * held
    subs = width // LANES
    step_groups = groups // steps
    pieces = model_width // (PIECE * LANES)
    long_masks, back_mask, ahead_mask, _ = masks
    plain = pl.BlockSpec((rows, width), lambda i: (0, i))
    placed = pl.BlockSpec((rows, width), lambda i: (0, first + i))
    anywhere = pl.BlockSpec(memory_space=pl.ANY)
    operands = [chip_in, link_in, filters, long_masks, back_mask, ahead_mask, mixed,
                cotangent, inputs, inputs, inputs, border, weights]
    in_specs = (
        [plain] * 2
        + [pl.BlockSpec((step_groups, taps), lambda i: (first + i, 0))]
        + [whole(mask.shape) for mask in (long_masks, back_mask, ahead_mask)]
        + [pl.BlockSpec((3, rows, width), lambda i: (0, 0, i)), placed]
        + branch_specs(rows, width, first, steps)
        + [whole(border.shape), whole(weights.shape)]
    )
    aliases = {}
    if so_far is not None:
        aliases = {len(operands) + n: n for n in range(len(so_far))}
        operands = operands + list(so_far)
        in_specs = in_specs + [anywhere] * len(so_far)
    return call(
        functools.partial(long_kernel, first=first, steps=steps, held=held),
        "long_parts",
        (held,),
        in_specs,
        [
            placed,
            pl.BlockSpec((3, subs // PIECE, 2 * PIECE, LANES), lambda i: (0, first + i, 0, 0)),
            pl.BlockSpec((3, 8, width), lambda i: (0, 0, first + i)),
            pl.BlockSpec((step_groups, taps), lambda i: (first + i, 0)),
            pl.BlockSpec((3, subs // PIECE, 3 * PIECE, LANES), lambda i: (0, first + i, 0, 0)),
            anywhere,
        ],
        [
            jax.ShapeDtypeStruct((rows, model_width), BF),
            jax.ShapeDtypeStruct((3, pieces, 2 * PIECE, LANES), F32),
            jax.ShapeDtypeStruct((3, 8, model_width), F32),
            jax.ShapeDtypeStruct((groups, taps), F32),
            jax.ShapeDtypeStruct((3, pieces, 3 * PIECE, LANES), F32),
            jax.ShapeDtypeStruct((rows, 3 * model_width), BF),
        ],
        (3 * groups * 2 * 128 * 256 * 256 // parts, 24 * 1024 * 1024 // parts),
        [
            pltpu.VMEM((subs, step_groups // subs, 8, taps), F32),
            pltpu.VMEM((2, 3, rows, width), BF),
            pltpu.SemaphoreType.DMA((2, 3)),
        ],
        aliases,
        32,
    )(*operands)


def last_rows_kernel(tail_ref, ahead_ref, w_ref, late_ref, old_ref, out_ref):
    lines = old_ref.shape[0]
    pieces = tail_ref.shape[2] // (PIECE * LANES)
    first_keep, second_keep = late_ref[0, :, 0:1], late_ref[1, :, 0:1]
    next_keep = late_ref[1, :, 1:2]
    for n in range(3 * pieces):
        b, piece = n // pieces, n % pieces
        first, second = [
            jnp.concatenate([ahead_ref[n, r * PIECE + u : r * PIECE + u + 1] for u in range(PIECE)], 1)
            for r in range(2)
        ]
        at = slice(n * PIECE * LANES, (n + 1) * PIECE * LANES)
        extra = w_ref[1:2, at] * (first_keep * first)
        extra = extra + w_ref[2:3, at] * (second_keep * first + next_keep * second)
        within = slice(piece * PIECE * LANES, (piece + 1) * PIECE * LANES)
        ending = (tail_ref[b, :, within] + extra).astype(BF)
        out_ref[:, at] = jnp.concatenate([old_ref[: lines // 2, at], ending], axis=0)


def finish_last_rows(grad_inputs, tail, ahead_rows, weights, late_mask):
    rows, total_width = grad_inputs.shape
    lines = 16
    held = pl.BlockSpec((lines, total_width), lambda i: (rows // lines - 1, 0))
    return call(
        last_rows_kernel,
        "last_rows",
        (1,),
        [whole(value.shape) for value in (tail, ahead_rows, weights, late_mask)] + [held],
        held,
        jax.ShapeDtypeStruct(grad_inputs.shape, BF),
        (1000000, 2000000),
        aliases={4: 0},
    )(tail, ahead_rows, weights, late_mask, grad_inputs)


def window_parts(value):
    count = lax.axis_size("dp")
    if count != 4:
        return [lax.psum(value, "dp")]
    return [value] + [swapped(value, "dp", bits) for bits in range(1, count)]


def from_next_chip(value):
    count = lax.axis_size("ctx")
    return lax.ppermute(value, "ctx", [(i, i - 1) for i in range(2, count, 2)])


def owned_sums(short_parts, long_parts, head):
    branches, pieces, short_rows, lanes = short_parts.shape
    groups, taps = long_parts.shape
    head_rows = head.shape[2]
    ctx_parts = lax.axis_size("ctx")
    total_pieces = branches * pieces
    head_flat = head.reshape(total_pieces * head_rows, lanes)
    if ctx_parts != 8 or total_pieces % ctx_parts or lanes != taps:
        weight_grad = short_parts.reshape(branches, pieces, 3, PIECE, lanes).transpose(2, 0, 1, 3, 4)
        weight_part = lax.psum_scatter(
            weight_grad.reshape(3, -1), "ctx", scatter_dimension=1, tiled=True
        )
        filter_part = lax.psum_scatter(long_parts, "ctx", scatter_dimension=0, tiled=True)
        weight_total, filter_total = lax.psum((weight_part, filter_part), "dp")
        return passed_along(head_flat, "ctx", -1), weight_total, filter_total
    held = total_pieces // ctx_parts
    chips = ctx_parts // 2
    short_owned = short_parts.reshape(ctx_parts, held * short_rows, lanes)
    long_owned = long_parts.reshape(ctx_parts, groups // ctx_parts, taps)
    joined = jnp.concatenate([short_owned, long_owned], axis=1)
    height = joined.shape[1]
    my_index = lax.axis_index("ctx")
    core, chip = my_index % 2, my_index // 2
    by_core = joined.reshape(chips, 2, height, lanes)
    kept = lax.dynamic_index_in_dim(by_core, core, 1, keepdims=False)
    given = lax.dynamic_index_in_dim(by_core, 1 - core, 1, keepdims=False)
    message = jnp.concatenate([given.reshape(chips * height, lanes), head_flat], axis=0)
    answer = swapped(message, "ctx", 1)
    paired = kept + answer[: chips * height].reshape(chips, height, lanes)
    partner_head = answer[chips * height :]
    mine = lax.dynamic_index_in_dim(paired, chip, 0, keepdims=False)
    rounded = paired.astype(BF)
    others = [
        swapped(lax.dynamic_index_in_dim(rounded, chip ^ d, 0, keepdims=False), "ctx", 2 * d)
        for d in range(1, chips)
    ]
    others = [value.astype(F32) for value in others]
    total = (mine + others[0]) + (others[1] + others[2])
    next_head = from_next_chip(head_flat.astype(BF)).astype(F32)
    ahead = jnp.where(core == 0, partner_head, next_head)
    return ahead, total, None


def finish_kernel(*refs, scales):
    *parts, short_ref, long_ref = refs
    values = [part[...] for part in parts]
    while len(values) > 1:
        values = [values[i] + values[i + 1] for i in range(0, len(values), 2)]
    total = values[0]
    held = short_ref.shape[1] // (PIECE * LANES)
    short_part = total[: held * 3 * PIECE] / scales[0]
    for piece in range(held):
        for j in range(3):
            for u in range(PIECE):
                row = (piece * 3 + j) * PIECE + u
                column = (piece * PIECE + u) * LANES
                short_ref[j : j + 1, column : column + LANES] = short_part[row : row + 1]
    long_ref[...] = total[held * 3 * PIECE :] / scales[1]


def finish(parts, held, scales):
    height, lanes = parts[0].shape
    shapes = [(3, held * PIECE * lanes), (height - held * 3 * PIECE, lanes)]
    return call(
        functools.partial(finish_kernel, scales=scales),
        "finish",
        (),
        [whole(part.shape) for part in parts],
        [whole(shape) for shape in shapes],
        [jax.ShapeDtypeStruct(shape, F32) for shape in shapes],
        (100000, 400000),
    )(*parts)


def local(projected, doc_ids, short_filter, long_filter, cotangent):
    grad_row = cotangent[0]
    seg_row = doc_ids[0]
    rows, model_width = grad_row.shape
    groups = long_filter.shape[0]
    short_taps = short_filter.shape[0]
    length = seg_row.shape[0]
    edge = short_taps - 1
    border = passed_along(projected[0, rows - edge :], "ctx", 1)
    filters = in_hbm(long_filter)
    masks = prepare(doc_ids, long_filter.shape[1])
    inputs_row, grad_row, short_filter = [
        in_hbm(value) for value in (projected[0], grad_row, short_filter)
    ]
    gated = []
    for part in range(PARTS):
        mixed, chip, link = make_gates(
            inputs_row, border, short_filter, grad_row, masks[1], part, PARTS
        )
        link_in = linked(link, "ctx")
        chip_in = swapped(chip, "ctx", 1)
        if part + 1 < PARTS:
            chip_in, link_in = in_hbm(chip_in), in_hbm(link_in)
        gated.append((mixed, chip_in, link_in))
    done = None
    for part, (mixed, chip_in, link_in) in enumerate(gated):
        done = make_long(
            chip_in, link_in, filters, masks, mixed, grad_row, inputs_row, border,
            short_filter, part, PARTS, done,
        )
    block_out, head, tail, long_parts, short_parts, grad_inputs = done
    norm_scale = lax.axis_size("dp") * length
    scales = (math.sqrt(norm_scale), math.sqrt(norm_scale * (model_width // groups)))
    ahead, total, filter_total = owned_sums(short_parts, long_parts, head)
    ahead = ahead.reshape(-1, 2 * PIECE, LANES)
    grad_inputs = finish_last_rows(grad_inputs, tail, ahead, short_filter, masks[3])
    if filter_total is None:
        held = 3 * model_width // (PIECE * LANES * lax.axis_size("ctx"))
        grad_short, grad_long = finish(window_parts(total), held, scales)
    else:
        grad_short, grad_long = total / scales[0], filter_total / scales[1]
    return (block_out[None], grad_inputs[None], grad_short, grad_long)


def solution(mesh):
    return jax.shard_map(
        local,
        mesh=mesh,
        in_specs=(P("dp", "ctx", None), P("dp", None), P(), P(), P("dp", "ctx", None)),
        out_specs=(P("dp", "ctx", None), P("dp", "ctx", None), P(None, "ctx"), P("ctx", None)),
        check_vma=False,
    )
```

```python
import functools
import math

import jax
import jax.numpy as jnp
from jax import lax
from jax.experimental import pallas as pl
from jax.experimental.pallas import tpu as pltpu
from jax.sharding import PartitionSpec as P

BF = jnp.bfloat16
F32 = jnp.float32
LANES = 128
EDGE = 16
WIDTH = 1024
GATE_WIDTH = 2048
PIECE = 4
PARTS = 2


def passed_along(value, axis, steps):
    count = lax.axis_size(axis)
    initial, last = (max(0, -steps), min(count, count - steps))
    return lax.ppermute(value, axis, [(source, source + steps) for source in range(initial, last)])


def swapped(value, axis, bits):
    count = lax.axis_size(axis)
    return lax.ppermute(value, axis, [(source, source ^ bits) for source in range(count)])


def linked(value, axis):
    count = lax.axis_size(axis)
    pairs = [(i, i + 1) for i in range(1, count - 1, 2)]
    return lax.ppermute(value, axis, pairs + [(b, a) for a, b in pairs])


def whole(shape):
    return pl.BlockSpec(shape, lambda *_: (0,) * len(shape))


def call(
    kernel, name, grid, in_specs, out_specs, out_shape, cost, scratch=(), aliases=None, mib=16
):
    return pl.pallas_call(
        kernel,
        name=name,
        grid=grid,
        in_specs=in_specs,
        out_specs=out_specs,
        out_shape=out_shape,
        scratch_shapes=list(scratch),
        input_output_aliases=aliases or {},
        compiler_params=pltpu.CompilerParams(vmem_limit_bytes=mib * 1024 * 1024),
        cost_estimate=pl.CostEstimate(flops=cost[0], bytes_accessed=cost[1], transcendentals=0),
    )


def in_hbm(value):
    return pltpu.with_memory_space_constraint(value, pltpu.HBM)


def prepare_kernel(
    ids_ref, far_x, far_cot, long_ref, back_ref, ahead_ref, late_ref, near_x, near_cot, sems
):
    held = near_cot.shape[1]
    copies = [
        pltpu.make_async_copy(
            far_x.at[:, b * far_cot.shape[1] : b * far_cot.shape[1] + held],
            near_x.at[:, b * held : (b + 1) * held],
            sems.at[b],
        )
        for b in range(3)
    ]
    copies.append(pltpu.make_async_copy(far_cot.at[:, :held], near_cot, sems.at[3]))
    for copy in copies:
        copy.start()
    taps = long_ref.shape[1]
    here = lax.axis_index("ctx")
    last = ids_ref.shape[1] // taps - 1

    def id_row(block, present):
        held = jnp.clip(block, 0, last) * taps
        row = ids_ref[:, pl.ds(pl.multiple_of(held, taps), taps)].astype(F32)
        return jnp.broadcast_to(jnp.where(present, row, -1.0), (taps, taps))

    prev_row = id_row(here - 1, here > 0)
    here_row = id_row(here, here >= 0)
    next_row = id_row(here + 1, here < last)
    here_col = jnp.transpose(here_row)
    prev_col = jnp.transpose(prev_row)
    rows = lax.broadcasted_iota(jnp.int32, (taps, taps), 0)
    cols = lax.broadcasted_iota(jnp.int32, (taps, taps), 1)

    def put(condition):
        return jnp.where(condition, 1.0, 0.0).astype(BF)

    same = here_col == here_row
    long_ref[0] = put((cols >= rows) & same)
    long_ref[1] = put((cols < rows) & (prev_col == here_row))
    long_ref[2] = put((cols < rows) & (here_col == next_row))
    long_ref[3] = put(((cols >= rows) & same) | ((cols < rows) & (here_col == next_row)))
    last_prev = here_col == pltpu.roll(prev_row, 2, 1)
    first_next = here_col == next_row
    for j in (1, 2):
        at = slice((j - 1) * taps, j * taps)
        back_ref[at, :taps] = put((cols == rows - j) & same)
        back_ref[at, taps:] = put((cols < 2) & (cols == rows + 2 - j) & last_prev)[:, :EDGE]
        ahead_ref[at, :] = put((cols == rows + j) & same)
        late = jnp.where((cols == rows + j - taps) & first_next, 1.0, 0.0)
        late_ref[j - 1] = late[taps - 8 :]
    for copy in copies:
        copy.wait()


def prepare(doc_ids, taps, inputs, cotangent, held):
    rows = inputs.shape[0]
    anywhere = pl.BlockSpec(memory_space=pl.ANY)
    shapes = [
        ((4, taps, taps), BF),
        ((2 * taps, taps + EDGE), BF),
        ((2 * taps, taps), BF),
        ((2, 8, taps), F32),
    ]
    return call(
        prepare_kernel,
        "prepare",
        (),
        [whole(doc_ids.shape), anywhere, anywhere],
        [whole(shape) for shape, _ in shapes] + [anywhere, anywhere],
        [jax.ShapeDtypeStruct(*entry) for entry in shapes]
        + [pltpu.VMEM((rows, 3 * held), BF), pltpu.VMEM((rows, held), BF)],
        (1000000, 4000000),
        [pltpu.SemaphoreType.DMA((4,))],
    )(in_hbm(doc_ids), in_hbm(inputs), in_hbm(cotangent))


def short_sum(weights, values, one, two):
    return (weights[0:1] * values.astype(F32) + weights[1:2] * one) + weights[2:3] * two


def gate_kernel(xq, xk, xv, edge_ref, w_ref, cot_ref, mask_ref, mixed_ref, chip_ref, link_ref,
                *, first, steps):
    rows, width = cot_ref.shape
    step = pl.program_id(0) + first
    mixed = []
    for b, x_ref in enumerate((xq, xk, xv)):
        values = x_ref[...]
        at = pl.ds(pl.multiple_of((step + b * steps) * width, width), width)
        edge = edge_ref[:, at]
        blank = jnp.zeros((EDGE - edge.shape[0], width), BF)
        both = jnp.dot(
            mask_ref[...],
            jnp.concatenate([values, edge, blank], axis=0),
            preferred_element_type=F32,
        )
        mixed.append(short_sum(w_ref[:, at], values, both[:rows], both[rows:]).astype(BF))
    for b in range(3):
        mixed_ref[b] = mixed[b]
    product = mixed[1] * mixed[2]
    grad_mix = cot_ref[...] * mixed[0]
    first_core = lax.axis_index("ctx") % 2 == 0
    chip_ref[...] = jnp.where(first_core, product, grad_mix)
    link_ref[...] = jnp.where(first_core, grad_mix, product)


def branch_specs(rows, width, first, steps):
    return [
        pl.BlockSpec((rows, width), lambda i, b=b: (0, first + i + b * steps)) for b in range(3)
    ]


def make_gates(inputs, border, weights, cotangent, back_mask, part, parts):
    rows = cotangent.shape[0]
    model_width = weights.shape[1] // 3
    width = GATE_WIDTH
    steps = model_width // width
    held = steps // parts
    first = part * held
    held_steps = cotangent.shape[1] // width
    held_first = first if held_steps == steps else 0
    plain = pl.BlockSpec((rows, width), lambda i: (0, i))
    return call(
        functools.partial(gate_kernel, first=first, steps=steps),
        "gates",
        (held,),
        branch_specs(rows, width, held_first, held_steps)
        + [
            whole(border.shape),
            whole(weights.shape),
            pl.BlockSpec((rows, width), lambda i: (0, held_first + i)),
            whole(back_mask.shape),
        ],
        [pl.BlockSpec((3, rows, width), lambda i: (0, 0, i)), plain, plain],
        [
            pltpu.VMEM((3, rows, held * width), BF),
            pltpu.VMEM((rows, held * width), BF),
            pltpu.VMEM((rows, held * width), BF),
        ],
        (2 * 256 * 256 * 3 * held * width, 9 * rows * held * width * 2),
        mib=32,
    )(inputs, inputs, inputs, border, weights, cotangent, back_mask)


def long_kernel(
    chip_in_ref, link_in_ref, filter_ref, long_ref, back_ref, ahead_ref,
    mixed_ref, cot_ref, xq, xk, xv, edge_ref, w_ref, *rest, first, steps, held,
):
    out_ref, head_ref, tail_ref, gl_ref, gs_ref, inputs_ref, diag, staged, sems = rest[-9:]
    rows_here, width = chip_in_ref.shape
    first_core = lax.axis_index("ctx") % 2 == 0
    taps = filter_ref.shape[1]
    subs = width // LANES
    per = filter_ref.shape[0] // subs
    share = LANES // per
    i = pl.program_id(0)
    slot = lax.rem(i, 2)
    lane_group = lax.broadcasted_iota(jnp.int32, (1, LANES), 1) // share
    lane = [jnp.where(lane_group == g, 1.0, 0.0).astype(BF) for g in range(per)]
    rows = lax.broadcasted_iota(jnp.int32, (8, taps), 0)
    cols = lax.broadcasted_iota(jnp.int32, (8, taps), 1)

    def column(step, b):
        return pl.ds(pl.multiple_of((step + first + b * steps) * width, width), width)

    def leaving(step, b):
        at = lax.rem(step, 2)
        target = out_ref.at[:, column(step, 0)] if b == 3 else inputs_ref.at[:, column(step, b)]
        return pltpu.make_async_copy(staged.at[at, b], target, sems.at[at, b])

    @pl.when(i >= 2)
    def _():
        for b in range(4):
            leaving(i - 2, b).wait()

    def both_sides(ls):
        here = mixed_ref[1, :, ls] * mixed_ref[2, :, ls]
        grad = cot_ref[:, ls] * mixed_ref[0, :, ls]
        chip_in, link_in = chip_in_ref[:, ls], link_in_ref[:, ls]
        sources = jnp.concatenate([here, jnp.where(first_core, link_in, chip_in)], axis=0)
        grads = jnp.concatenate([grad, jnp.where(first_core, chip_in, link_in)], axis=0)
        return sources, grads

    mixed_grads = [[], [], []]
    for u in range(subs):
        ls = slice(u * LANES, (u + 1) * LANES)
        gs = slice(u * per, (u + 1) * per)
        sources, grads = both_sides(ls)
        filters = filter_ref[gs].astype(F32)
        turned = [
            pltpu.roll(
                jnp.broadcast_to(filters[g : g + 1], (taps, taps)), 0, 1, stride=1, stride_axis=0
            ).astype(BF)
            for g in range(per)
        ]
        near = [part * long_ref[0] for part in turned]

        def long_conv(far, stacked, dims):
            across = jnp.transpose(stacked)
            parts = []
            for g in range(per):
                taken = across[g * share : (g + 1) * share]
                right = jnp.concatenate([near[g], turned[g] * long_ref[far]], axis=dims)
                parts.append(
                    lax.dot_general(
                        taken, right, (((1,), (dims,)), ((), ())), preferred_element_type=F32
                    )
                )
            return jnp.transpose(jnp.concatenate(parts, axis=0).astype(BF))

        long_mix = long_conv(1, sources, 0)
        grad_product = long_conv(2, grads, 1)
        staged[slot, 3, :, ls] = mixed_ref[0, :, ls] * long_mix
        mixed_grads[0].append(cot_ref[:, ls] * long_mix)
        mixed_grads[1].append(grad_product * mixed_ref[2, :, ls])
        mixed_grads[2].append(grad_product * mixed_ref[1, :, ls])

    leaving(i, 3).start()
    edge_keep = back_ref[:, taps : taps + 2].astype(F32)
    for b, x_ref in enumerate((xq, xk, xv)):
        mixed_grad = jnp.concatenate(mixed_grads[b], axis=1)
        first_rows = mixed_grad[:16].astype(F32)
        for u in range(subs):
            for r in range(2):
                at_row = r * PIECE + u % PIECE
                head_ref[b, u // PIECE, at_row : at_row + 1, :] = first_rows[
                    r : r + 1, u * LANES : (u + 1) * LANES
                ]
        both = jnp.dot(ahead_ref[...], mixed_grad, preferred_element_type=F32)
        one, two = both[:rows_here], both[rows_here:]
        at = column(i, b)
        total = short_sum(w_ref[:, at], mixed_grad, one, two)
        tail_ref[b] = total[rows_here - 8 :]
        staged[slot, b] = total.astype(BF)
        leaving(i, b).start()
        values = x_ref[...].astype(F32)
        edge = edge_ref[:, at].astype(F32)
        over_edge = (
            None,
            edge_keep[0:1, 1:2] * first_rows[0:1] * edge[1:2],
            edge_keep[taps : taps + 1, 0:1] * first_rows[0:1] * edge[0:1]
            + edge_keep[taps + 1 : taps + 2, 1:2] * first_rows[1:2] * edge[1:2],
        )
        for j, part in enumerate((mixed_grad.astype(F32), one, two)):
            summed = jnp.sum(values * part, axis=0, keepdims=True)
            if j:
                summed = summed + over_edge[j]
            for u in range(subs):
                at_row = j * PIECE + u % PIECE
                gs_ref[b, u // PIECE, at_row : at_row + 1, :] = summed[
                    :, u * LANES : (u + 1) * LANES
                ]

    for u in range(subs):
        ls = slice(u * LANES, (u + 1) * LANES)
        gs = slice(u * per, (u + 1) * per)
        sources, grads = both_sides(ls)
        here = sources[:rows_here]
        spread = jnp.concatenate([here * lane[g] for g in range(per)], axis=0)
        inner = lax.dot_general(
            spread, grads, (((1,), (1,)), ((), ())), preferred_element_type=F32
        ).reshape(per, taps // 8, 8, 2 * taps)
        keep = long_ref[3].astype(F32)
        total = None
        for k in range(taps // 8):
            nearer = (cols >= rows + 8 * k)[None]
            term = jnp.where(nearer, inner[:, k, :, :taps], inner[:, k, :, taps:])
            term = (term * keep[8 * k : 8 * k + 8][None]).reshape(per * 8, taps)
            if k:
                term = pltpu.roll(term, taps - 8 * k, 1)
            total = term if total is None else total + term
        diag[u] = total.reshape(per, 8, taps)
        lined = diag[u, :, 0, :]
        for r in range(1, 8):
            lined = lined + pltpu.roll(diag[u, :, r, :], taps - r, 1)
        gl_ref[gs, :] = lined

    @pl.when(i == held - 1)
    def _():
        for b in range(4):
            if held > 1:
                leaving(i - 1, b).wait()
            leaving(i, b).wait()


def make_long(chip_in, link_in, filters, masks, mixed, cotangent, inputs, border,
              weights, part, parts, so_far):
    rows, model_width = cotangent.shape
    groups, taps = filters.shape
    width = WIDTH
    steps = model_width // width
    held = steps // parts
    first = part * held
    subs = width // LANES
    step_groups = groups // steps
    pieces = model_width // (PIECE * LANES)
    long_masks, back_mask, ahead_mask, _ = masks
    plain = pl.BlockSpec((rows, width), lambda i: (0, i))
    placed = pl.BlockSpec((rows, width), lambda i: (0, first + i))
    anywhere = pl.BlockSpec(memory_space=pl.ANY)
    operands = [chip_in, link_in, filters, long_masks, back_mask, ahead_mask, mixed,
                cotangent, inputs, inputs, inputs, border, weights]
    in_specs = (
        [plain] * 2
        + [pl.BlockSpec((step_groups, taps), lambda i: (first + i, 0))]
        + [whole(mask.shape) for mask in (long_masks, back_mask, ahead_mask)]
        + [pl.BlockSpec((3, rows, width), lambda i: (0, 0, i)), placed]
        + branch_specs(rows, width, first, steps)
        + [whole(border.shape), whole(weights.shape)]
    )
    aliases = {}
    if so_far is not None:
        aliases = {len(operands) + n: n for n in range(len(so_far))}
        operands = operands + list(so_far)
        in_specs = in_specs + [anywhere] * len(so_far)
    return call(
        functools.partial(long_kernel, first=first, steps=steps, held=held),
        "long_parts",
        (held,),
        in_specs,
        [
            anywhere,
            pl.BlockSpec((3, subs // PIECE, 2 * PIECE, LANES), lambda i: (0, first + i, 0, 0)),
            pl.BlockSpec((3, 8, width), lambda i: (0, 0, first + i)),
            pl.BlockSpec((step_groups, taps), lambda i: (first + i, 0)),
            pl.BlockSpec((3, subs // PIECE, 3 * PIECE, LANES), lambda i: (0, first + i, 0, 0)),
            anywhere,
        ],
        [
            jax.ShapeDtypeStruct((rows, model_width), BF),
            jax.ShapeDtypeStruct((3, pieces, 2 * PIECE, LANES), F32),
            jax.ShapeDtypeStruct((3, 8, model_width), F32),
            jax.ShapeDtypeStruct((groups, taps), F32),
            jax.ShapeDtypeStruct((3, pieces, 3 * PIECE, LANES), F32),
            jax.ShapeDtypeStruct((rows, 3 * model_width), BF),
        ],
        (3 * groups * 2 * 128 * 256 * 256 // parts, 24 * 1024 * 1024 // parts),
        [
            pltpu.VMEM((subs, step_groups // subs, 8, taps), F32),
            pltpu.VMEM((2, 4, rows, width), BF),
            pltpu.SemaphoreType.DMA((2, 4)),
        ],
        aliases,
        32,
    )(*operands)


def last_rows_kernel(tail_ref, ahead_ref, w_ref, late_ref, old_ref, out_ref):
    lines = old_ref.shape[0]
    pieces = tail_ref.shape[2] // (PIECE * LANES)
    first_keep, second_keep = late_ref[0, :, 0:1], late_ref[1, :, 0:1]
    next_keep = late_ref[1, :, 1:2]
    for n in range(3 * pieces):
        b, piece = n // pieces, n % pieces
        first, second = [
            jnp.concatenate([ahead_ref[n, r * PIECE + u : r * PIECE + u + 1] for u in range(PIECE)], 1)
            for r in range(2)
        ]
        at = slice(n * PIECE * LANES, (n + 1) * PIECE * LANES)
        extra = w_ref[1:2, at] * (first_keep * first)
        extra = extra + w_ref[2:3, at] * (second_keep * first + next_keep * second)
        within = slice(piece * PIECE * LANES, (piece + 1) * PIECE * LANES)
        ending = (tail_ref[b, :, within] + extra).astype(BF)
        out_ref[:, at] = jnp.concatenate([old_ref[: lines // 2, at], ending], axis=0)


def finish_last_rows(grad_inputs, tail, ahead_rows, weights, late_mask):
    rows, total_width = grad_inputs.shape
    lines = 16
    held = pl.BlockSpec((lines, total_width), lambda i: (rows // lines - 1, 0))
    return call(
        last_rows_kernel,
        "last_rows",
        (1,),
        [whole(value.shape) for value in (tail, ahead_rows, weights, late_mask)] + [held],
        held,
        jax.ShapeDtypeStruct(grad_inputs.shape, BF),
        (1000000, 2000000),
        aliases={4: 0},
    )(tail, ahead_rows, weights, late_mask, grad_inputs)


def window_parts(value):
    count = lax.axis_size("dp")
    if count != 4:
        return [lax.psum(value, "dp")]
    return [value] + [swapped(value, "dp", bits) for bits in range(1, count)]


def from_next_chip(value):
    count = lax.axis_size("ctx")
    return lax.ppermute(value, "ctx", [(i, i - 1) for i in range(2, count, 2)])


def owned_sums(short_parts, long_parts, head):
    branches, pieces, short_rows, lanes = short_parts.shape
    groups, taps = long_parts.shape
    head_rows = head.shape[2]
    ctx_parts = lax.axis_size("ctx")
    total_pieces = branches * pieces
    head_flat = head.reshape(total_pieces * head_rows, lanes)
    if ctx_parts != 8 or total_pieces % ctx_parts or lanes != taps:
        weight_grad = short_parts.reshape(branches, pieces, 3, PIECE, lanes).transpose(2, 0, 1, 3, 4)
        weight_part = lax.psum_scatter(
            weight_grad.reshape(3, -1), "ctx", scatter_dimension=1, tiled=True
        )
        filter_part = lax.psum_scatter(long_parts, "ctx", scatter_dimension=0, tiled=True)
        weight_total, filter_total = lax.psum((weight_part, filter_part), "dp")
        return passed_along(head_flat, "ctx", -1), weight_total, filter_total
    held = total_pieces // ctx_parts
    chips = ctx_parts // 2
    short_owned = short_parts.reshape(ctx_parts, held * short_rows, lanes)
    long_owned = long_parts.reshape(ctx_parts, groups // ctx_parts, taps)
    joined = jnp.concatenate([short_owned, long_owned], axis=1)
    height = joined.shape[1]
    my_index = lax.axis_index("ctx")
    core, chip = my_index % 2, my_index // 2
    by_core = joined.reshape(chips, 2, height, lanes)
    kept = lax.dynamic_index_in_dim(by_core, core, 1, keepdims=False)
    given = lax.dynamic_index_in_dim(by_core, 1 - core, 1, keepdims=False)
    message = jnp.concatenate([given.reshape(chips * height, lanes), head_flat], axis=0)
    answer = swapped(message, "ctx", 1)
    paired = kept + answer[: chips * height].reshape(chips, height, lanes)
    partner_head = answer[chips * height :]
    mine = lax.dynamic_index_in_dim(paired, chip, 0, keepdims=False)
    rounded = paired.astype(BF)
    others = [
        swapped(lax.dynamic_index_in_dim(rounded, chip ^ d, 0, keepdims=False), "ctx", 2 * d)
        for d in range(1, chips)
    ]
    others = [value.astype(F32) for value in others]
    total = (mine + others[0]) + (others[1] + others[2])
    next_head = from_next_chip(head_flat.astype(BF)).astype(F32)
    ahead = jnp.where(core == 0, partner_head, next_head)
    return ahead, total, None


def finish_kernel(*refs, scales):
    *parts, short_ref, long_ref = refs
    values = [part[...] for part in parts]
    while len(values) > 1:
        values = [values[i] + values[i + 1] for i in range(0, len(values), 2)]
    total = values[0]
    held = short_ref.shape[1] // (PIECE * LANES)
    short_part = total[: held * 3 * PIECE] / scales[0]
    for piece in range(held):
        for j in range(3):
            for u in range(PIECE):
                row = (piece * 3 + j) * PIECE + u
                column = (piece * PIECE + u) * LANES
                short_ref[j : j + 1, column : column + LANES] = short_part[row : row + 1]
    long_ref[...] = total[held * 3 * PIECE :] / scales[1]


def finish(parts, held, scales):
    height, lanes = parts[0].shape
    shapes = [(3, held * PIECE * lanes), (height - held * 3 * PIECE, lanes)]
    return call(
        functools.partial(finish_kernel, scales=scales),
        "finish",
        (),
        [whole(part.shape) for part in parts],
        [whole(shape) for shape in shapes],
        [jax.ShapeDtypeStruct(shape, F32) for shape in shapes],
        (100000, 400000),
    )(*parts)


def local(projected, doc_ids, short_filter, long_filter, cotangent):
    grad_row = cotangent[0]
    seg_row = doc_ids[0]
    rows, model_width = grad_row.shape
    groups = long_filter.shape[0]
    short_taps = short_filter.shape[0]
    length = seg_row.shape[0]
    edge = short_taps - 1
    border = passed_along(projected[0, rows - edge :], "ctx", 1)
    filters = in_hbm(long_filter)
    *masks, early_x, early_cot = prepare(
        doc_ids, long_filter.shape[1], projected[0], grad_row, model_width // PARTS
    )
    inputs_row, grad_row, short_filter = [
        in_hbm(value) for value in (projected[0], grad_row, short_filter)
    ]
    gated = []
    for part in range(PARTS):
        mixed, chip, link = make_gates(
            inputs_row if part else early_x, border, short_filter,
            grad_row if part else early_cot, masks[1], part, PARTS,
        )
        link_in = linked(link, "ctx")
        chip_in = swapped(chip, "ctx", 1)
        if part + 1 < PARTS:
            chip_in, link_in = in_hbm(chip_in), in_hbm(link_in)
        gated.append((mixed, chip_in, link_in))
    done = None
    for part, (mixed, chip_in, link_in) in enumerate(gated):
        done = make_long(
            chip_in, link_in, filters, masks, mixed, grad_row, inputs_row, border,
            short_filter, part, PARTS, done,
        )
    block_out, head, tail, long_parts, short_parts, grad_inputs = done
    norm_scale = lax.axis_size("dp") * length
    scales = (math.sqrt(norm_scale), math.sqrt(norm_scale * (model_width // groups)))
    ahead, total, filter_total = owned_sums(short_parts, long_parts, head)
    ahead = ahead.reshape(-1, 2 * PIECE, LANES)
    grad_inputs = finish_last_rows(grad_inputs, tail, ahead, short_filter, masks[3])
    if filter_total is None:
        held = 3 * model_width // (PIECE * LANES * lax.axis_size("ctx"))
        grad_short, grad_long = finish(window_parts(total), held, scales)
    else:
        grad_short, grad_long = total / scales[0], filter_total / scales[1]
    return (block_out[None], grad_inputs[None], grad_short, grad_long)


def solution(mesh):
    return jax.shard_map(
        local,
        mesh=mesh,
        in_specs=(P("dp", "ctx", None), P("dp", None), P(), P(), P("dp", "ctx", None)),
        out_specs=(P("dp", "ctx", None), P("dp", "ctx", None), P(None, "ctx"), P("ctx", None)),
        check_vma=False,
    )
```

```python
import functools
import math

import jax
import jax.numpy as jnp
from jax import lax
from jax.experimental import pallas as pl
from jax.experimental.pallas import tpu as pltpu
from jax.sharding import PartitionSpec as P

BF = jnp.bfloat16
F32 = jnp.float32
LANES = 128
EDGE = 16
WIDTH = 1024
GATE_WIDTH = 2048
PIECE = 4
PARTS = 2


def passed_along(value, axis, steps):
    count = lax.axis_size(axis)
    initial, last = (max(0, -steps), min(count, count - steps))
    return lax.ppermute(value, axis, [(source, source + steps) for source in range(initial, last)])


def swapped(value, axis, bits):
    count = lax.axis_size(axis)
    return lax.ppermute(value, axis, [(source, source ^ bits) for source in range(count)])


def linked(value, axis):
    count = lax.axis_size(axis)
    pairs = [(i, i + 1) for i in range(1, count - 1, 2)]
    return lax.ppermute(value, axis, pairs + [(b, a) for a, b in pairs])


def whole(shape):
    return pl.BlockSpec(shape, lambda *_: (0,) * len(shape))


def call(
    kernel, name, grid, in_specs, out_specs, out_shape, cost, scratch=(), aliases=None, mib=16
):
    return pl.pallas_call(
        kernel,
        name=name,
        grid=grid,
        in_specs=in_specs,
        out_specs=out_specs,
        out_shape=out_shape,
        scratch_shapes=list(scratch),
        input_output_aliases=aliases or {},
        compiler_params=pltpu.CompilerParams(vmem_limit_bytes=mib * 1024 * 1024),
        cost_estimate=pl.CostEstimate(flops=cost[0], bytes_accessed=cost[1], transcendentals=0),
    )


def in_hbm(value):
    return pltpu.with_memory_space_constraint(value, pltpu.HBM)


def prepare_kernel(
    ids_ref, far_x, far_cot, far_w, long_ref, back_ref, ahead_ref, late_ref,
    near_x, near_cot, near_w, sems,
):
    held = near_cot.shape[1]
    copies = [
        pltpu.make_async_copy(
            far_x.at[:, b * far_cot.shape[1] : b * far_cot.shape[1] + held],
            near_x.at[:, b * held : (b + 1) * held],
            sems.at[b],
        )
        for b in range(3)
    ]
    copies.append(pltpu.make_async_copy(far_cot.at[:, :held], near_cot, sems.at[3]))
    copies.append(pltpu.make_async_copy(far_w, near_w, sems.at[4]))
    for copy in copies:
        copy.start()
    taps = long_ref.shape[1]
    here = lax.axis_index("ctx")
    last = ids_ref.shape[1] // taps - 1

    def id_row(block, present):
        held = jnp.clip(block, 0, last) * taps
        row = ids_ref[:, pl.ds(pl.multiple_of(held, taps), taps)].astype(F32)
        return jnp.broadcast_to(jnp.where(present, row, -1.0), (taps, taps))

    prev_row = id_row(here - 1, here > 0)
    here_row = id_row(here, here >= 0)
    next_row = id_row(here + 1, here < last)
    here_col = jnp.transpose(here_row)
    prev_col = jnp.transpose(prev_row)
    rows = lax.broadcasted_iota(jnp.int32, (taps, taps), 0)
    cols = lax.broadcasted_iota(jnp.int32, (taps, taps), 1)

    def put(condition):
        return jnp.where(condition, 1.0, 0.0).astype(BF)

    same = here_col == here_row
    long_ref[0] = put((cols >= rows) & same)
    long_ref[1] = put((cols < rows) & (prev_col == here_row))
    long_ref[2] = put((cols < rows) & (here_col == next_row))
    long_ref[3] = put(((cols >= rows) & same) | ((cols < rows) & (here_col == next_row)))
    last_prev = here_col == pltpu.roll(prev_row, 2, 1)
    first_next = here_col == next_row
    for j in (1, 2):
        at = slice((j - 1) * taps, j * taps)
        back_ref[at, :taps] = put((cols == rows - j) & same)
        back_ref[at, taps:] = put((cols < 2) & (cols == rows + 2 - j) & last_prev)[:, :EDGE]
        ahead_ref[at, :] = put((cols == rows + j) & same)
        late = jnp.where((cols == rows + j - taps) & first_next, 1.0, 0.0)
        late_ref[j - 1] = late[taps - 8 :]
    for copy in copies:
        copy.wait()


def prepare(doc_ids, taps, inputs, cotangent, weights, held):
    rows = inputs.shape[0]
    anywhere = pl.BlockSpec(memory_space=pl.ANY)
    shapes = [
        ((4, taps, taps), BF),
        ((2 * taps, taps + EDGE), BF),
        ((2 * taps, taps), BF),
        ((2, 8, taps), F32),
    ]
    return call(
        prepare_kernel,
        "prepare",
        (),
        [whole(doc_ids.shape), anywhere, anywhere, anywhere],
        [whole(shape) for shape, _ in shapes] + [anywhere, anywhere, anywhere],
        [jax.ShapeDtypeStruct(*entry) for entry in shapes]
        + [pltpu.VMEM((rows, 3 * held), BF), pltpu.VMEM((rows, held), BF)]
        + [pltpu.VMEM(weights.shape, F32)],
        (1000000, 4000000),
        [pltpu.SemaphoreType.DMA((5,))],
    )(in_hbm(doc_ids), in_hbm(inputs), in_hbm(cotangent), in_hbm(weights))


def short_sum(weights, values, one, two):
    return (weights[0:1] * values.astype(F32) + weights[1:2] * one) + weights[2:3] * two


def gate_kernel(xq, xk, xv, edge_ref, w_ref, cot_ref, mask_ref, mixed_ref, chip_ref, link_ref,
                *, first, steps):
    rows, width = cot_ref.shape
    step = pl.program_id(0) + first
    mixed = []
    for b, x_ref in enumerate((xq, xk, xv)):
        values = x_ref[...]
        at = pl.ds(pl.multiple_of((step + b * steps) * width, width), width)
        edge = edge_ref[:, at]
        blank = jnp.zeros((EDGE - edge.shape[0], width), BF)
        both = jnp.dot(
            mask_ref[...],
            jnp.concatenate([values, edge, blank], axis=0),
            preferred_element_type=F32,
        )
        mixed.append(short_sum(w_ref[:, at], values, both[:rows], both[rows:]).astype(BF))
    for b in range(3):
        mixed_ref[b] = mixed[b]
    product = mixed[1] * mixed[2]
    grad_mix = cot_ref[...] * mixed[0]
    first_core = lax.axis_index("ctx") % 2 == 0
    chip_ref[...] = jnp.where(first_core, product, grad_mix)
    link_ref[...] = jnp.where(first_core, grad_mix, product)


def branch_specs(rows, width, first, steps):
    return [
        pl.BlockSpec((rows, width), lambda i, b=b: (0, first + i + b * steps)) for b in range(3)
    ]


def make_gates(inputs, border, weights, cotangent, back_mask, part, parts):
    rows = cotangent.shape[0]
    model_width = weights.shape[1] // 3
    width = GATE_WIDTH
    steps = model_width // width
    held = steps // parts
    first = part * held
    held_steps = cotangent.shape[1] // width
    held_first = first if held_steps == steps else 0
    plain = pl.BlockSpec((rows, width), lambda i: (0, i))
    return call(
        functools.partial(gate_kernel, first=first, steps=steps),
        "gates",
        (held,),
        branch_specs(rows, width, held_first, held_steps)
        + [
            whole(border.shape),
            whole(weights.shape),
            pl.BlockSpec((rows, width), lambda i: (0, held_first + i)),
            whole(back_mask.shape),
        ],
        [pl.BlockSpec((3, rows, width), lambda i: (0, 0, i)), plain, plain],
        [
            pltpu.VMEM((3, rows, held * width), BF),
            pltpu.VMEM((rows, held * width), BF),
            pltpu.VMEM((rows, held * width), BF),
        ],
        (2 * 256 * 256 * 3 * held * width, 9 * rows * held * width * 2),
        mib=32,
    )(inputs, inputs, inputs, border, weights, cotangent, back_mask)


def long_kernel(
    chip_in_ref, link_in_ref, filter_ref, long_ref, back_ref, ahead_ref,
    mixed_ref, cot_ref, xq, xk, xv, edge_ref, w_ref, *rest, first, steps, held,
):
    out_ref, head_ref, tail_ref, gl_ref, gs_ref, inputs_ref, diag, staged, sems = rest[-9:]
    rows_here, width = chip_in_ref.shape
    first_core = lax.axis_index("ctx") % 2 == 0
    taps = filter_ref.shape[1]
    subs = width // LANES
    per = filter_ref.shape[0] // subs
    share = LANES // per
    i = pl.program_id(0)
    slot = lax.rem(i, 2)
    lane_group = lax.broadcasted_iota(jnp.int32, (1, LANES), 1) // share
    lane = [jnp.where(lane_group == g, 1.0, 0.0).astype(BF) for g in range(per)]
    rows = lax.broadcasted_iota(jnp.int32, (8, taps), 0)
    cols = lax.broadcasted_iota(jnp.int32, (8, taps), 1)

    def column(step, b):
        return pl.ds(pl.multiple_of((step + first + b * steps) * width, width), width)

    def leaving(step, b):
        at = lax.rem(step, 2)
        target = out_ref.at[:, column(step, 0)] if b == 3 else inputs_ref.at[:, column(step, b)]
        return pltpu.make_async_copy(staged.at[at, b], target, sems.at[at, b])

    @pl.when(i >= 2)
    def _():
        for b in range(4):
            leaving(i - 2, b).wait()

    def both_sides(ls):
        here = mixed_ref[1, :, ls] * mixed_ref[2, :, ls]
        grad = cot_ref[:, ls] * mixed_ref[0, :, ls]
        chip_in, link_in = chip_in_ref[:, ls], link_in_ref[:, ls]
        sources = jnp.concatenate([here, jnp.where(first_core, link_in, chip_in)], axis=0)
        grads = jnp.concatenate([grad, jnp.where(first_core, chip_in, link_in)], axis=0)
        return sources, grads

    mixed_grads = [[], [], []]
    for u in range(subs):
        ls = slice(u * LANES, (u + 1) * LANES)
        gs = slice(u * per, (u + 1) * per)
        sources, grads = both_sides(ls)
        filters = filter_ref[gs].astype(F32)
        turned = [
            pltpu.roll(
                jnp.broadcast_to(filters[g : g + 1], (taps, taps)), 0, 1, stride=1, stride_axis=0
            ).astype(BF)
            for g in range(per)
        ]
        near = [part * long_ref[0] for part in turned]

        def long_conv(far, stacked, dims):
            across = jnp.transpose(stacked)
            parts = []
            for g in range(per):
                taken = across[g * share : (g + 1) * share]
                right = jnp.concatenate([near[g], turned[g] * long_ref[far]], axis=dims)
                parts.append(
                    lax.dot_general(
                        taken, right, (((1,), (dims,)), ((), ())), preferred_element_type=F32
                    )
                )
            return jnp.transpose(jnp.concatenate(parts, axis=0).astype(BF))

        long_mix = long_conv(1, sources, 0)
        grad_product = long_conv(2, grads, 1)
        staged[slot, 3, :, ls] = mixed_ref[0, :, ls] * long_mix
        mixed_grads[0].append(cot_ref[:, ls] * long_mix)
        mixed_grads[1].append(grad_product * mixed_ref[2, :, ls])
        mixed_grads[2].append(grad_product * mixed_ref[1, :, ls])

    leaving(i, 3).start()
    edge_keep = back_ref[:, taps : taps + 2].astype(F32)
    for b, x_ref in enumerate((xq, xk, xv)):
        mixed_grad = jnp.concatenate(mixed_grads[b], axis=1)
        first_rows = mixed_grad[:16].astype(F32)
        for u in range(subs):
            for r in range(2):
                at_row = r * PIECE + u % PIECE
                head_ref[b, u // PIECE, at_row : at_row + 1, :] = first_rows[
                    r : r + 1, u * LANES : (u + 1) * LANES
                ]
        both = jnp.dot(ahead_ref[...], mixed_grad, preferred_element_type=F32)
        one, two = both[:rows_here], both[rows_here:]
        at = column(i, b)
        total = short_sum(w_ref[:, at], mixed_grad, one, two)
        tail_ref[b] = total[rows_here - 8 :]
        staged[slot, b] = total.astype(BF)
        leaving(i, b).start()
        values = x_ref[...].astype(F32)
        edge = edge_ref[:, at].astype(F32)
        over_edge = (
            None,
            edge_keep[0:1, 1:2] * first_rows[0:1] * edge[1:2],
            edge_keep[taps : taps + 1, 0:1] * first_rows[0:1] * edge[0:1]
            + edge_keep[taps + 1 : taps + 2, 1:2] * first_rows[1:2] * edge[1:2],
        )
        for j, part in enumerate((mixed_grad.astype(F32), one, two)):
            summed = jnp.sum(values * part, axis=0, keepdims=True)
            if j:
                summed = summed + over_edge[j]
            for u in range(subs):
                at_row = j * PIECE + u % PIECE
                gs_ref[b, u // PIECE, at_row : at_row + 1, :] = summed[
                    :, u * LANES : (u + 1) * LANES
                ]

    for u in range(subs):
        ls = slice(u * LANES, (u + 1) * LANES)
        gs = slice(u * per, (u + 1) * per)
        sources, grads = both_sides(ls)
        here = sources[:rows_here]
        spread = jnp.concatenate([here * lane[g] for g in range(per)], axis=0)
        inner = lax.dot_general(
            spread, grads, (((1,), (1,)), ((), ())), preferred_element_type=F32
        ).reshape(per, taps // 8, 8, 2 * taps)
        keep = long_ref[3].astype(F32)
        total = None
        for k in range(taps // 8):
            nearer = (cols >= rows + 8 * k)[None]
            term = jnp.where(nearer, inner[:, k, :, :taps], inner[:, k, :, taps:])
            term = (term * keep[8 * k : 8 * k + 8][None]).reshape(per * 8, taps)
            if k:
                term = pltpu.roll(term, taps - 8 * k, 1)
            total = term if total is None else total + term
        diag[u] = total.reshape(per, 8, taps)
        lined = diag[u, :, 0, :]
        for r in range(1, 8):
            lined = lined + pltpu.roll(diag[u, :, r, :], taps - r, 1)
        gl_ref[gs, :] = lined

    @pl.when(i == held - 1)
    def _():
        for b in range(4):
            if held > 1:
                leaving(i - 1, b).wait()
            leaving(i, b).wait()


def make_long(chip_in, link_in, filters, masks, mixed, cotangent, inputs, border,
              weights, part, parts, so_far):
    rows, model_width = cotangent.shape
    groups, taps = filters.shape
    width = WIDTH
    steps = model_width // width
    held = steps // parts
    first = part * held
    subs = width // LANES
    step_groups = groups // steps
    pieces = model_width // (PIECE * LANES)
    long_masks, back_mask, ahead_mask, _ = masks
    plain = pl.BlockSpec((rows, width), lambda i: (0, i))
    placed = pl.BlockSpec((rows, width), lambda i: (0, first + i))
    anywhere = pl.BlockSpec(memory_space=pl.ANY)
    operands = [chip_in, link_in, filters, long_masks, back_mask, ahead_mask, mixed,
                cotangent, inputs, inputs, inputs, border, weights]
    in_specs = (
        [plain] * 2
        + [pl.BlockSpec((step_groups, taps), lambda i: (first + i, 0))]
        + [whole(mask.shape) for mask in (long_masks, back_mask, ahead_mask)]
        + [pl.BlockSpec((3, rows, width), lambda i: (0, 0, i)), placed]
        + branch_specs(rows, width, first, steps)
        + [whole(border.shape), whole(weights.shape)]
    )
    aliases = {}
    if so_far is not None:
        aliases = {len(operands) + n: n for n in range(len(so_far))}
        operands = operands + list(so_far)
        in_specs = in_specs + [anywhere] * len(so_far)
    return call(
        functools.partial(long_kernel, first=first, steps=steps, held=held),
        "long_parts",
        (held,),
        in_specs,
        [
            anywhere,
            pl.BlockSpec((3, subs // PIECE, 2 * PIECE, LANES), lambda i: (0, first + i, 0, 0)),
            pl.BlockSpec((3, 8, width), lambda i: (0, 0, first + i)),
            pl.BlockSpec((step_groups, taps), lambda i: (first + i, 0)),
            pl.BlockSpec((3, subs // PIECE, 3 * PIECE, LANES), lambda i: (0, first + i, 0, 0)),
            anywhere,
        ],
        [
            jax.ShapeDtypeStruct((rows, model_width), BF),
            jax.ShapeDtypeStruct((3, pieces, 2 * PIECE, LANES), F32),
            jax.ShapeDtypeStruct((3, 8, model_width), F32),
            jax.ShapeDtypeStruct((groups, taps), F32),
            jax.ShapeDtypeStruct((3, pieces, 3 * PIECE, LANES), F32),
            jax.ShapeDtypeStruct((rows, 3 * model_width), BF),
        ],
        (3 * groups * 2 * 128 * 256 * 256 // parts, 24 * 1024 * 1024 // parts),
        [
            pltpu.VMEM((subs, step_groups // subs, 8, taps), F32),
            pltpu.VMEM((2, 4, rows, width), BF),
            pltpu.SemaphoreType.DMA((2, 4)),
        ],
        aliases,
        32,
    )(*operands)


def last_rows_kernel(tail_ref, ahead_ref, w_ref, late_ref, old_ref, out_ref):
    lines = old_ref.shape[0]
    pieces = tail_ref.shape[2] // (PIECE * LANES)
    first_keep, second_keep = late_ref[0, :, 0:1], late_ref[1, :, 0:1]
    next_keep = late_ref[1, :, 1:2]
    for n in range(3 * pieces):
        b, piece = n // pieces, n % pieces
        first, second = [
            jnp.concatenate([ahead_ref[n, r * PIECE + u : r * PIECE + u + 1] for u in range(PIECE)], 1)
            for r in range(2)
        ]
        at = slice(n * PIECE * LANES, (n + 1) * PIECE * LANES)
        extra = w_ref[1:2, at] * (first_keep * first)
        extra = extra + w_ref[2:3, at] * (second_keep * first + next_keep * second)
        within = slice(piece * PIECE * LANES, (piece + 1) * PIECE * LANES)
        ending = (tail_ref[b, :, within] + extra).astype(BF)
        out_ref[:, at] = jnp.concatenate([old_ref[: lines // 2, at], ending], axis=0)


def finish_last_rows(grad_inputs, tail, ahead_rows, weights, late_mask):
    rows, total_width = grad_inputs.shape
    lines = 16
    held = pl.BlockSpec((lines, total_width), lambda i: (rows // lines - 1, 0))
    return call(
        last_rows_kernel,
        "last_rows",
        (1,),
        [whole(value.shape) for value in (tail, ahead_rows, weights, late_mask)] + [held],
        held,
        jax.ShapeDtypeStruct(grad_inputs.shape, BF),
        (1000000, 2000000),
        aliases={4: 0},
    )(tail, ahead_rows, weights, late_mask, grad_inputs)


def window_parts(value):
    count = lax.axis_size("dp")
    if count != 4:
        return [lax.psum(value, "dp")]
    return [value] + [swapped(value, "dp", bits) for bits in range(1, count)]


def from_next_chip(value):
    count = lax.axis_size("ctx")
    return lax.ppermute(value, "ctx", [(i, i - 1) for i in range(2, count, 2)])


def owned_sums(short_parts, long_parts, head):
    branches, pieces, short_rows, lanes = short_parts.shape
    groups, taps = long_parts.shape
    head_rows = head.shape[2]
    ctx_parts = lax.axis_size("ctx")
    total_pieces = branches * pieces
    head_flat = head.reshape(total_pieces * head_rows, lanes)
    if ctx_parts != 8 or total_pieces % ctx_parts or lanes != taps:
        weight_grad = short_parts.reshape(branches, pieces, 3, PIECE, lanes).transpose(2, 0, 1, 3, 4)
        weight_part = lax.psum_scatter(
            weight_grad.reshape(3, -1), "ctx", scatter_dimension=1, tiled=True
        )
        filter_part = lax.psum_scatter(long_parts, "ctx", scatter_dimension=0, tiled=True)
        weight_total, filter_total = lax.psum((weight_part, filter_part), "dp")
        return passed_along(head_flat, "ctx", -1), weight_total, filter_total
    held = total_pieces // ctx_parts
    chips = ctx_parts // 2
    short_owned = short_parts.reshape(ctx_parts, held * short_rows, lanes)
    long_owned = long_parts.reshape(ctx_parts, groups // ctx_parts, taps)
    joined = jnp.concatenate([short_owned, long_owned], axis=1)
    height = joined.shape[1]
    my_index = lax.axis_index("ctx")
    core, chip = my_index % 2, my_index // 2
    by_core = joined.reshape(chips, 2, height, lanes)
    kept = lax.dynamic_index_in_dim(by_core, core, 1, keepdims=False)
    given = lax.dynamic_index_in_dim(by_core, 1 - core, 1, keepdims=False)
    message = jnp.concatenate([given.reshape(chips * height, lanes), head_flat], axis=0)
    answer = swapped(message, "ctx", 1)
    paired = kept + answer[: chips * height].reshape(chips, height, lanes)
    partner_head = answer[chips * height :]
    mine = lax.dynamic_index_in_dim(paired, chip, 0, keepdims=False)
    rounded = paired.astype(BF)
    others = [
        swapped(lax.dynamic_index_in_dim(rounded, chip ^ d, 0, keepdims=False), "ctx", 2 * d)
        for d in range(1, chips)
    ]
    others = [value.astype(F32) for value in others]
    total = (mine + others[0]) + (others[1] + others[2])
    next_head = from_next_chip(head_flat.astype(BF)).astype(F32)
    ahead = jnp.where(core == 0, partner_head, next_head)
    return ahead, total, None


def finish_kernel(*refs, scales):
    *parts, short_ref, long_ref = refs
    values = [part[...] for part in parts]
    while len(values) > 1:
        values = [values[i] + values[i + 1] for i in range(0, len(values), 2)]
    total = values[0]
    held = short_ref.shape[1] // (PIECE * LANES)
    short_part = total[: held * 3 * PIECE] / scales[0]
    for piece in range(held):
        for j in range(3):
            for u in range(PIECE):
                row = (piece * 3 + j) * PIECE + u
                column = (piece * PIECE + u) * LANES
                short_ref[j : j + 1, column : column + LANES] = short_part[row : row + 1]
    long_ref[...] = total[held * 3 * PIECE :] / scales[1]


def finish(parts, held, scales):
    height, lanes = parts[0].shape
    shapes = [(3, held * PIECE * lanes), (height - held * 3 * PIECE, lanes)]
    return call(
        functools.partial(finish_kernel, scales=scales),
        "finish",
        (),
        [whole(part.shape) for part in parts],
        [whole(shape) for shape in shapes],
        [jax.ShapeDtypeStruct(shape, F32) for shape in shapes],
        (100000, 400000),
    )(*parts)


def local(projected, doc_ids, short_filter, long_filter, cotangent):
    grad_row = cotangent[0]
    seg_row = doc_ids[0]
    rows, model_width = grad_row.shape
    groups = long_filter.shape[0]
    short_taps = short_filter.shape[0]
    length = seg_row.shape[0]
    edge = short_taps - 1
    border = passed_along(projected[0, rows - edge :], "ctx", 1)
    filters = in_hbm(long_filter)
    *masks, early_x, early_cot, early_w = prepare(
        doc_ids, long_filter.shape[1], projected[0], grad_row, short_filter, model_width // PARTS
    )
    inputs_row, grad_row, short_filter = [
        in_hbm(value) for value in (projected[0], grad_row, short_filter)
    ]
    gated = []
    for part in range(PARTS):
        mixed, chip, link = make_gates(
            inputs_row if part else early_x, border, early_w,
            grad_row if part else early_cot, masks[1], part, PARTS,
        )
        link_in = linked(link, "ctx")
        chip_in = swapped(chip, "ctx", 1)
        if part + 1 < PARTS:
            chip_in, link_in = in_hbm(chip_in), in_hbm(link_in)
        gated.append((mixed, chip_in, link_in))
    done = None
    for part, (mixed, chip_in, link_in) in enumerate(gated):
        done = make_long(
            chip_in, link_in, filters, masks, mixed, grad_row, inputs_row, border,
            early_w, part, PARTS, done,
        )
    block_out, head, tail, long_parts, short_parts, grad_inputs = done
    norm_scale = lax.axis_size("dp") * length
    scales = (math.sqrt(norm_scale), math.sqrt(norm_scale * (model_width // groups)))
    ahead, total, filter_total = owned_sums(short_parts, long_parts, head)
    ahead = ahead.reshape(-1, 2 * PIECE, LANES)
    grad_inputs = finish_last_rows(grad_inputs, tail, ahead, early_w, masks[3])
    if filter_total is None:
        held = 3 * model_width // (PIECE * LANES * lax.axis_size("ctx"))
        grad_short, grad_long = finish(window_parts(total), held, scales)
    else:
        grad_short, grad_long = total / scales[0], filter_total / scales[1]
    return (block_out[None], grad_inputs[None], grad_short, grad_long)


def solution(mesh):
    return jax.shard_map(
        local,
        mesh=mesh,
        in_specs=(P("dp", "ctx", None), P("dp", None), P(), P(), P("dp", "ctx", None)),
        out_specs=(P("dp", "ctx", None), P("dp", "ctx", None), P(None, "ctx"), P("ctx", None)),
        check_vma=False,
    )
```
